256 devices in a mesh: space: 32 (over z_lo, x, y), chan: 8 (over z_hi, core).
Axes of the slice: x: 4, y: 4, z: 8 (z_hi: 4, z_lo: 2; z = z_hi * 2 + z_lo), core: 2. Of those that a mesh axis runs over, the one named last changes fastest.
Arguments:
- volume: bfloat16 [128, 32, 64, 128], P('chan', 'space'), may hold values from -6 to 6
- weight_one: bfloat16 [27, 128, 128], replicated, may hold values from -0.109375 to 0.109375
- bias_one: float32 [128], replicated, may hold values from -3 to 3
- weight_two: bfloat16 [27, 128, 128], replicated, may hold values from -0.109375 to 0.109375
- bias_two: float32 [128], replicated, may hold values from -3 to 3
Outputs:
- features: bfloat16 [128, 32, 64, 128], P('chan', 'space')
The draws below stay inside these ranges and needn't reach their ends.
All inputs are finite; a program needn't handle non-finite values.
Results may differ from the reference program's by a relative error of at most 0.0045.
Values may be sent and summed in bfloat16 or wider, within the bound.
No kernel may reach another device: no remote copies, remote signals or barrier semaphores. Data moves between devices by JAX's collectives and lax.ppermute only.
A program may use at most 64 MiB of HBM per device.

```python
import jax
import jax.numpy as jnp
from jax import lax

C = 128
TAPS = 27
Y = 64
Z = 128
NX = 32


def block_scale(own_key, extent, split, smallest, largest):
    def one(position, parts):
        steps = jax.random.uniform(jax.random.fold_in(jax.random.fold_in(own_key, 6), position), (parts,), jnp.float32, smallest / len(split), largest / len(split))
        return jnp.repeat(jnp.exp(steps), extent[position] // parts).reshape((-1,) + (1,) * (len(extent) - position - 1))

    loudness = one(*split[0])
    for cut in split[1:]:
        loudness = loudness * one(*cut)
    return loudness


def gaussian(own_key, shape, scale, most, shards=(), kind=jnp.bfloat16):
    entries = scale * jax.random.normal(own_key, shape, jnp.float32)
    if shards:
        entries = entries * block_scale(own_key, shape, shards, -0.22, 0.18)
    return jnp.clip(entries, -most, most).astype(kind)


def setup_inputs(seed: int = 0) -> dict:
    seeds = jax.random.split(jax.random.key(seed), 6)
    volume = gaussian(seeds[0], (C, NX, Y, Z), 1.0, 6.0, ((0, 8), (1, 32)))
    weight_one = gaussian(seeds[1], (TAPS, C, C), (TAPS * C) ** -0.5, 0.109375)
    bias_one = gaussian(seeds[2], (C,), 0.5, 3.0, (), jnp.float32)
    weight_two = gaussian(seeds[3], (TAPS, C, C), (TAPS * C) ** -0.5, 0.109375)
    bias_two = gaussian(seeds[4], (C,), 0.5, 3.0, (), jnp.float32)
    return {"volume": volume, "weight_one": weight_one, "bias_one": bias_one, "weight_two": weight_two, "bias_two": bias_two}


def conv_layer(volume, kernel, offsets):
    shaped = kernel.reshape(3, 3, 3, kernel.shape[1], kernel.shape[2]).astype(jnp.float32)
    summed = lax.conv_general_dilated(
        volume[None].astype(jnp.float32), shaped, (1, 1, 1), ((1, 1), (1, 1), (1, 1)),
        dimension_numbers=("NCDHW", "DHWIO", "NCDHW"), precision=lax.Precision.HIGHEST)[0]
    return jax.nn.relu(summed + offsets[:, None, None, None]).astype(jnp.bfloat16)


def reference(volume, weight_one, bias_one, weight_two, bias_two):
    hidden = conv_layer(volume, weight_one, bias_one)
    return conv_layer(hidden, weight_two, bias_two)
```

```python
import jax
import jax.numpy as jnp
from jax import lax
from jax.experimental import pallas as pl
from jax.experimental.pallas import tpu as pltpu
from jax.sharding import PartitionSpec as P

BF16 = jnp.bfloat16
F32 = jnp.float32


def along_lanes(total, lanes):
    chans = total.shape[0] // 3
    lane = lax.broadcasted_iota(jnp.int32, (chans, lanes), 1)
    low = pltpu.roll(total[:chans], 1, 1)
    high = pltpu.roll(total[2 * chans :], lanes - 1, 1)
    return (
        total[chans : 2 * chans]
        + jnp.where(lane == 0, 0.0, low)
        + jnp.where(lane == lanes - 1, 0.0, high)
    )


def conv_rows(get, weight, bias, store, rows, lanes):
    for start in range(0, rows, 2):
        parts = []
        for a in range(3):
            for e in range(3):
                pair = [get(a, start + e + n) for n in range(2)]
                parts.append(jnp.concatenate(pair, axis=1))
        stacked = jnp.concatenate(parts, axis=0)
        total = jnp.dot(weight, stacked, preferred_element_type=F32)
        for n in range(2):
            u = along_lanes(total[:, n * lanes : (n + 1) * lanes], lanes)
            store(start + n, jnp.maximum(u + bias, 0.0))


def first_kernel(block_ref, before_ref, own_ref, after_ref, weight_ref, bias_ref, out_ref):
    refs = (before_ref, own_ref, after_ref)
    groups = own_ref.shape[0]
    rows, _, lanes = out_ref.shape
    block = block_ref[0]

    def get(a, row):
        return jnp.concatenate([refs[a][g, row] for g in range(groups)], axis=0)

    def store(row, value):
        if row == 0:
            value = jnp.where(block == 0, 0.0, value)
        if row == rows - 1:
            value = jnp.where(block == block_ref[1] - 1, 0.0, value)
        out_ref[row] = value.astype(BF16)

    conv_rows(get, weight_ref[...], bias_ref[...], store, rows, lanes)


def second_kernel(before_ref, own_ref, after_ref, weight_ref, bias_ref, out_ref):
    refs = (before_ref, own_ref, after_ref)
    cores, groups, rows, width, lanes = out_ref.shape

    def get(a, row):
        return refs[a][row]

    def store(row, value):
        value = value.astype(BF16)
        for g in range(groups):
            for c in range(cores):
                at = (g * cores + c) * width
                out_ref[c, g, row] = value[at : at + width]

    conv_rows(get, weight_ref[...], bias_ref[...], store, rows, lanes)


def arranged(weight):
    _, inner, outer = weight.shape
    taps = weight.reshape(9, 3, inner, outer)
    return taps.transpose(1, 3, 0, 2).reshape(3 * outer, 9 * inner)


def solution(mesh):
    space = mesh.shape["space"]
    chan = mesh.shape["chan"]
    cores = 2
    groups = chan // cores
    up = [(i, i + 1) for i in range(space - 1)]
    down = [(i + 1, i) for i in range(space - 1)]
    swap = [(i, i ^ 1) for i in range(chan)]

    def ahead(k):
        return [(i, (i + cores * k) % chan) for i in range(chan)]

    vmem = pl.BlockSpec(memory_space=pltpu.VMEM)
    smem = pl.BlockSpec(memory_space=pltpu.SMEM)

    def per_device(volume, weight_one, bias_one, weight_two, bias_two):
        width, _, length, lanes = volume.shape
        full = width * chan
        rows = length // chan
        index = lax.axis_index("chan")
        group, core = index // cores, index % cores

        one = arranged(weight_one)
        two = arranged(weight_two)

        flat = volume[:, 0].transpose(1, 0, 2)
        flat = jnp.pad(flat, ((2, 2), (0, 0), (0, 0)))
        blocks = jnp.stack([flat[rows * i : rows * i + rows + 4] for i in range(chan)])
        blocks = blocks.reshape(groups, cores, rows + 4, width, lanes)
        mine = lax.dynamic_index_in_dim(blocks, core, 1, keepdims=False)
        theirs = lax.dynamic_index_in_dim(blocks, 1 - core, 1, keepdims=False)
        swapped = lax.ppermute(theirs, "chan", swap)
        first = jnp.where(core == 0, mine, swapped)
        second = jnp.where(core == 0, swapped, mine)
        both = jnp.concatenate([first, second], axis=2)
        whole = both
        for k in range(1, groups):
            sent = lax.dynamic_index_in_dim(both, (group + k) % groups, 0, keepdims=True)
            got = lax.ppermute(sent, "chan", ahead(k))
            whole = lax.dynamic_update_slice_in_dim(whole, got, (group + groups - k) % groups, 0)

        before = lax.ppermute(whole, "space", up)
        after = lax.ppermute(whole, "space", down)
        where = jnp.stack([index.astype(jnp.int32), jnp.int32(chan)])
        hidden = pl.pallas_call(
            first_kernel,
            out_shape=jax.ShapeDtypeStruct((rows + 2, full, lanes), BF16),
            in_specs=[smem] + [vmem] * 5,
            out_specs=vmem,
            name="first_layer",
        )(where, before, whole, after, one, bias_one[:, None])

        before = lax.ppermute(hidden, "space", up)
        after = lax.ppermute(hidden, "space", down)
        out = pl.pallas_call(
            second_kernel,
            out_shape=jax.ShapeDtypeStruct((cores, groups, rows, width, lanes), BF16),
            in_specs=[vmem] * 5,
            out_specs=vmem,
            name="second_layer",
        )(before, hidden, after, two, bias_two[:, None])

        back = out
        for k in range(1, groups):
            sent = lax.dynamic_index_in_dim(out, (group + k) % groups, 1, keepdims=True)
            got = lax.ppermute(sent, "chan", ahead(k))
            back = lax.dynamic_update_slice_in_dim(back, got, (group + groups - k) % groups, 1)
        mine = lax.dynamic_index_in_dim(back, core, 0, keepdims=False)
        theirs = lax.dynamic_index_in_dim(back, 1 - core, 0, keepdims=False)
        swapped = lax.ppermute(theirs, "chan", swap)
        first = jnp.where(core == 0, mine, swapped)
        second = jnp.where(core == 0, swapped, mine)
        features = jnp.stack([first, second], axis=1).reshape(length, width, lanes)
        return features.transpose(1, 0, 2)[:, None]

    placed = (P("chan", "space", None, None), P(), P(), P(), P())
    return jax.shard_map(
        per_device,
        mesh=mesh,
        in_specs=placed,
        out_specs=P("chan", "space", None, None),
        check_vma=False,
    )
```

```python
import jax
import jax.numpy as jnp
from jax import lax
from jax.experimental import pallas as pl
from jax.experimental.pallas import tpu as pltpu
from jax.sharding import PartitionSpec as P

BF16 = jnp.bfloat16
F32 = jnp.float32
CORES = 2
RIM = 2
PARAMS = pltpu.CompilerParams(vmem_limit_bytes=24 * 1024 * 1024)
VMEM = pl.BlockSpec(memory_space=pltpu.VMEM)
SMEM = pl.BlockSpec(memory_space=pltpu.SMEM)


def along_lanes(total, lanes):
    chans = total.shape[0] // 3
    lane = lax.broadcasted_iota(jnp.int32, (chans, lanes), 1)
    low = pltpu.roll(total[:chans], 1, 1)
    high = pltpu.roll(total[2 * chans :], lanes - 1, 1)
    return (
        total[chans : 2 * chans]
        + jnp.where(lane == 0, 0.0, low)
        + jnp.where(lane == lanes - 1, 0.0, high)
    )


def conv_rows(get, planes, weight, store, rows, lanes):
    for start in range(0, rows, 2):
        parts = []
        for a in range(planes):
            for e in range(3):
                pair = [get(a, start + e + n) for n in range(2)]
                parts.append(jnp.concatenate(pair, axis=1))
        stacked = jnp.concatenate(parts, axis=0)
        total = jnp.dot(weight, stacked, preferred_element_type=F32)
        for n in range(2):
            store(start + n, along_lanes(total[:, n * lanes : (n + 1) * lanes], lanes))


def pack_kernel(place_ref, volume_ref, mine_ref, theirs_ref, rows_ref):
    width, _, length, lanes = volume_ref.shape
    groups = mine_ref.shape[0]
    rows = length // (groups * CORES)
    edge = jnp.zeros((RIM, width, lanes), BF16)
    rows_ref[:RIM] = edge
    rows_ref[RIM + length :] = edge
    turned = jnp.swapaxes(volume_ref[:, 0].astype(F32), 0, 1)
    rows_ref[RIM : RIM + length] = turned.astype(BF16)
    group, core = place_ref[0], place_ref[1]
    for k in range(groups):
        target = lax.rem(group + k, groups) * CORES
        mine_ref[k] = rows_ref[pl.ds((target + core) * rows, rows + 2 * RIM)]
        theirs_ref[k] = rows_ref[pl.ds((target + 1 - core) * rows, rows + 2 * RIM)]


def own_kernel(own_ref, weight_ref, out_ref):
    rows, _, lanes = out_ref.shape

    def get(_, row):
        if len(own_ref.shape) == 3:
            return own_ref[row]
        return jnp.concatenate([own_ref[g, row] for g in range(own_ref.shape[0])], axis=0)

    def store(row, value):
        out_ref[row] = value

    conv_rows(get, 1, weight_ref[...], store, rows, lanes)


def reader(place_ref, before_ref, after_ref):
    outside = (place_ref[2] == 0, place_ref[2] == place_ref[3] - 1)
    refs = (before_ref, after_ref)

    def get(a, row):
        ref = refs[a]
        if len(ref.shape) == 3:
            value = ref[row]
        else:
            value = jnp.concatenate([ref[g, row] for g in range(ref.shape[0])], axis=0)
        return jnp.where(outside[a], jnp.zeros_like(value), value)

    return get


def first_kernel(place_ref, before_ref, after_ref, own_ref, weight_ref, bias_ref, out_ref):
    rows, _, lanes = out_ref.shape
    group, core = place_ref[0], place_ref[1]
    block = group * CORES + core
    bias = bias_ref[...]

    def store(row, value):
        value = jnp.maximum(value + own_ref[row] + bias, 0.0)
        if row == 0:
            value = jnp.where(block == 0, 0.0, value)
        if row == rows - 1:
            value = jnp.where(block == place_ref[4] - 1, 0.0, value)
        out_ref[row] = value.astype(BF16)

    get = reader(place_ref, before_ref, after_ref)
    conv_rows(get, 2, weight_ref[...], store, rows, lanes)


def second_kernel(place_ref, before_ref, after_ref, own_ref, weight_ref, bias_ref, *refs):
    outs, all_ref = refs[:-1], refs[-1]
    groups, cores, rows, width, lanes = all_ref.shape
    bias = bias_ref[...]

    def store(row, value):
        value = jnp.maximum(value + own_ref[row] + bias, 0.0).astype(BF16)
        for g in range(groups):
            for c in range(cores):
                at = (g * cores + c) * width
                all_ref[g, c, row] = value[at : at + width]

    get = reader(place_ref, before_ref, after_ref)
    conv_rows(get, 2, weight_ref[...], store, rows, lanes)
    for k in range(groups):
        outs[k][...] = all_ref[lax.rem(place_ref[0] + k, groups)]


def unpack_kernel(place_ref, swapped_ref, *refs):
    blocks, out_ref, rows_ref = refs[:-2], refs[-2], refs[-1]
    groups = len(blocks)
    _, rows, width, lanes = blocks[0].shape
    group, core = place_ref[0], place_ref[1]
    for k in range(groups):
        source = lax.rem(group + groups - k, groups) * CORES
        rows_ref[source + core] = blocks[k][core]
        rows_ref[source + 1 - core] = swapped_ref[k]
    length = groups * CORES * rows
    turned = rows_ref[...].reshape(length, width, lanes).astype(F32)
    out_ref[:, 0] = jnp.swapaxes(turned, 0, 1).astype(BF16)


def arranged(weight):
    _, inner, outer = weight.shape
    taps = weight.reshape(3, 3, 3, inner, outer)
    own = taps[1].transpose(1, 3, 0, 2).reshape(3 * outer, 3 * inner)
    beside = taps[::2].transpose(2, 4, 0, 1, 3).reshape(3 * outer, 6 * inner)
    return own, beside


def cost(rows, planes, full, lanes):
    flops = 2 * rows * lanes * full * full * 9 * planes
    return pl.CostEstimate(flops=flops, bytes_accessed=4_000_000, transcendentals=0)


def solution(mesh):
    space = mesh.shape["space"]
    chan = mesh.shape["chan"]
    groups = chan // CORES
    up = [(i, (i + 1) % space) for i in range(space)]
    down = [(i, (i + space - 1) % space) for i in range(space)]
    swap = [(i, i ^ 1) for i in range(chan)]

    def ahead(k):
        return [(i, (i + CORES * k) % chan) for i in range(chan)]

    def call(kernel, shapes, inputs, scratch=(), **kwargs):
        single = not isinstance(shapes, list)
        return pl.pallas_call(
            kernel,
            out_shape=shapes,
            in_specs=[SMEM if x.ndim == 1 else VMEM for x in inputs],
            out_specs=VMEM if single else [VMEM] * len(shapes),
            scratch_shapes=scratch,
            compiler_params=PARAMS,
            **kwargs,
        )(*inputs)

    def per_device(volume, weight_one, bias_one, weight_two, bias_two):
        width, _, length, lanes = volume.shape
        full = width * chan
        rows = length // chan
        index = lax.axis_index("chan")
        plane = lax.axis_index("space")
        group, core = index // CORES, index % CORES
        place = jnp.stack([group, core, plane, jnp.int32(space), jnp.int32(chan)]).astype(jnp.int32)

        own_one, beside_one = arranged(weight_one)
        own_two, beside_two = arranged(weight_two)

        piece = jax.ShapeDtypeStruct((groups, rows + 2 * RIM, width, lanes), BF16)
        mine, theirs = call(
            pack_kernel,
            [piece, piece],
            [place, volume],
            [pltpu.VMEM((length + 2 * RIM, width, lanes), BF16)],
            name="pack_rows",
        )
        swapped = lax.ppermute(theirs, "chan", swap)
        first = jnp.where(core == 0, mine, swapped)
        second = jnp.where(core == 0, swapped, mine)
        both = jnp.concatenate([first, second], axis=2)
        whole = jnp.zeros_like(both)
        whole = lax.dynamic_update_slice_in_dim(whole, both[:1], group, 0)
        for k in range(1, groups):
            got = lax.ppermute(both[k : k + 1], "chan", ahead(k))
            whole = lax.dynamic_update_slice_in_dim(whole, got, (group + groups - k) % groups, 0)

        before = lax.ppermute(whole, "space", up)
        after = lax.ppermute(whole, "space", down)
        own = call(
            own_kernel,
            jax.ShapeDtypeStruct((rows + RIM, full, lanes), F32),
            [whole, own_one],
            cost_estimate=cost(rows + RIM, 1, full, lanes),
            name="first_own",
        )
        hidden = call(
            first_kernel,
            jax.ShapeDtypeStruct((rows + RIM, full, lanes), BF16),
            [place, before, after, own, beside_one, bias_one[:, None]],
            cost_estimate=cost(rows + RIM, 2, full, lanes),
            name="first_layer",
        )

        before = lax.ppermute(hidden, "space", up)
        after = lax.ppermute(hidden, "space", down)
        own = call(
            own_kernel,
            jax.ShapeDtypeStruct((rows, full, lanes), F32),
            [hidden, own_two],
            cost_estimate=cost(rows, 1, full, lanes),
            name="second_own",
        )
        blocks = call(
            second_kernel,
            [jax.ShapeDtypeStruct((CORES, rows, width, lanes), BF16)] * groups,
            [place, before, after, own, beside_two, bias_two[:, None]],
            [pltpu.VMEM((groups, CORES, rows, width, lanes), BF16)],
            cost_estimate=cost(rows, 2, full, lanes),
            name="second_layer",
        )

        blocks = [blocks[0]] + [lax.ppermute(blocks[k], "chan", ahead(k)) for k in range(1, groups)]
        theirs = jnp.stack([lax.dynamic_index_in_dim(b, 1 - core, 0, keepdims=False) for b in blocks])
        swapped = lax.ppermute(theirs, "chan", swap)
        return call(
            unpack_kernel,
            jax.ShapeDtypeStruct(volume.shape, BF16),
            [place, swapped, *blocks],
            [pltpu.VMEM((chan, rows, width, lanes), BF16)],
            name="unpack_rows",
        )

    placed = (P("chan", "space", None, None), P(), P(), P(), P())
    return jax.shard_map(
        per_device,
        mesh=mesh,
        in_specs=placed,
        out_specs=P("chan", "space", None, None),
        check_vma=False,
    )
```

```python
import jax
import jax.numpy as jnp
from jax import lax
from jax.experimental import pallas as pl
from jax.experimental.pallas import tpu as pltpu
from jax.sharding import PartitionSpec as P

BF16 = jnp.bfloat16
F32 = jnp.float32
CORES = 2
RIM = 2
PARAMS = pltpu.CompilerParams(vmem_limit_bytes=24 * 1024 * 1024)
VMEM = pl.BlockSpec(memory_space=pltpu.VMEM)
SMEM = pl.BlockSpec(memory_space=pltpu.SMEM)


def along_lanes(total, lanes):
    chans = total.shape[0] // 3
    lane = lax.broadcasted_iota(jnp.int32, (chans, lanes), 1)
    low = pltpu.roll(total[:chans], 1, 1)
    high = pltpu.roll(total[2 * chans :], lanes - 1, 1)
    return (
        total[chans : 2 * chans]
        + jnp.where(lane == 0, 0.0, low)
        + jnp.where(lane == lanes - 1, 0.0, high)
    )


def conv_rows(get, planes, weight, store, rows, lanes):
    for start in range(0, rows, 2):
        parts = []
        for a in range(planes):
            for e in range(3):
                pair = [get(a, start + e + n) for n in range(2)]
                parts.append(jnp.concatenate(pair, axis=1))
        stacked = jnp.concatenate(parts, axis=0)
        total = jnp.dot(weight, stacked, preferred_element_type=F32)
        for n in range(2):
            store(start + n, along_lanes(total[:, n * lanes : (n + 1) * lanes], lanes))


def pack_kernel(place_ref, volume_ref, *refs):
    outs, rows_ref = refs[:-1], refs[-1]
    width, _, length, lanes = volume_ref.shape
    groups = len(outs)
    rows = length // groups
    edge = jnp.zeros((RIM, width, lanes), BF16)
    rows_ref[:RIM] = edge
    rows_ref[RIM + length :] = edge
    turned = jnp.swapaxes(volume_ref[:, 0].astype(F32), 0, 1)
    rows_ref[RIM : RIM + length] = turned.astype(BF16)
    for k in range(groups):
        target = lax.rem(place_ref[0] + k, groups)
        outs[k][0] = rows_ref[pl.ds(target * rows, rows + 2 * RIM)]


def gather_rows(place_ref, kept_ref, other_ref, joined_ref, outside=None):
    core = place_ref[1]
    groups, rows, width, lanes = other_ref.shape
    offset = core * (kept_ref.shape[1] - rows)
    for row in range(rows):
        parts = []
        for g in range(groups):
            kept = kept_ref[g, offset + row]
            other = other_ref[g, row]
            parts += [jnp.where(core == 0, kept, other), jnp.where(core == 0, other, kept)]
        joined = jnp.concatenate(parts, axis=0)
        if outside is not None:
            joined = jnp.where(outside, jnp.zeros_like(joined), joined)
        joined_ref[row] = joined


def first_own_kernel(place_ref, kept_ref, other_ref, weight_ref, later_ref, bias_ref, out_ref, core_ref, joined_ref):
    core_ref[0] = place_ref[1]
    gather_rows(place_ref, kept_ref, other_ref, joined_ref)
    second_own_kernel(joined_ref, weight_ref, out_ref)


def second_own_kernel(own_ref, weight_ref, out_ref):
    rows, _, lanes = out_ref.shape

    def get(_, row):
        return own_ref[row]

    def store(row, value):
        out_ref[row] = value

    conv_rows(get, 1, weight_ref[...], store, rows, lanes)


def outside_of(place_ref):
    return place_ref[2] == 0, place_ref[2] == place_ref[3] - 1


def first_kernel(
    place_ref, before_ref, before_other_ref, after_ref, after_other_ref, own_ref, weight_ref, bias_ref, out_ref, joined_ref
):
    rows, _, lanes = out_ref.shape
    block = place_ref[0] * CORES + place_ref[1]
    bias = bias_ref[...]
    outside = outside_of(place_ref)
    gather_rows(place_ref, before_ref, before_other_ref, joined_ref.at[0], outside[0])
    gather_rows(place_ref, after_ref, after_other_ref, joined_ref.at[1], outside[1])

    def get(a, row):
        return joined_ref[a, row]

    def store(row, value):
        value = jnp.maximum(value + own_ref[row] + bias, 0.0)
        if row == 0:
            value = jnp.where(block == 0, 0.0, value)
        if row == rows - 1:
            value = jnp.where(block == place_ref[4] - 1, 0.0, value)
        out_ref[row] = value.astype(BF16)

    conv_rows(get, 2, weight_ref[...], store, rows, lanes)


def second_kernel(place_ref, before_ref, after_ref, own_ref, weight_ref, bias_ref, *refs):
    outs, all_ref = refs[:-1], refs[-1]
    groups, cores, rows, width, lanes = all_ref.shape
    bias = bias_ref[...]

    def store(row, value):
        value = jnp.maximum(value + own_ref[row] + bias, 0.0).astype(BF16)
        for g in range(groups):
            for c in range(cores):
                at = (g * cores + c) * width
                all_ref[g, c, row] = value[at : at + width]

    beside = (before_ref, after_ref)
    outside = outside_of(place_ref)

    def get(a, row):
        value = beside[a][row]
        return jnp.where(outside[a], jnp.zeros_like(value), value)

    conv_rows(get, 2, weight_ref[...], store, rows, lanes)
    for k in range(groups):
        outs[k][...] = all_ref[lax.rem(place_ref[0] + k, groups)]


def unpack_kernel(place_ref, swapped_ref, *refs):
    blocks, out_ref, rows_ref = refs[:-2], refs[-2], refs[-1]
    groups = len(blocks)
    _, rows, width, lanes = blocks[0].shape
    group, core = place_ref[0], place_ref[1]
    for k in range(groups):
        source = lax.rem(group + groups - k, groups) * CORES
        rows_ref[source + core] = blocks[k][core]
        rows_ref[source + 1 - core] = swapped_ref[k]
    length = groups * CORES * rows
    turned = rows_ref[...].reshape(length, width, lanes).astype(F32)
    out_ref[:, 0] = jnp.swapaxes(turned, 0, 1).astype(BF16)


def arranged(weight):
    _, inner, outer = weight.shape
    taps = weight.reshape(3, 3, 3, inner, outer)
    own = taps[1].transpose(1, 3, 0, 2).reshape(3 * outer, 3 * inner)
    beside = taps[::2].transpose(2, 4, 0, 1, 3).reshape(3 * outer, 6 * inner)
    return own, beside


def cost(rows, planes, full, lanes):
    flops = 2 * rows * lanes * full * full * 9 * planes
    return pl.CostEstimate(flops=flops, bytes_accessed=4_000_000, transcendentals=0)


def solution(mesh):
    space = mesh.shape["space"]
    chan = mesh.shape["chan"]
    groups = chan // CORES
    up = [(i, (i + 1) % space) for i in range(space)]
    down = [(i, (i + space - 1) % space) for i in range(space)]
    swap = [(i, i ^ 1) for i in range(chan)]

    def ahead(k):
        return [(i, (i + CORES * k) % chan) for i in range(chan)]

    def call(kernel, shapes, inputs, scratch=(), **kwargs):
        single = not isinstance(shapes, list)
        return pl.pallas_call(
            kernel,
            out_shape=shapes,
            in_specs=[SMEM if x.ndim == 1 else VMEM for x in inputs],
            out_specs=VMEM if single else [SMEM if len(x.shape) == 1 else VMEM for x in shapes],
            scratch_shapes=scratch,
            compiler_params=PARAMS,
            **kwargs,
        )(*inputs)

    def per_device(volume, weight_one, bias_one, weight_two, bias_two):
        width, _, length, lanes = volume.shape
        full = width * chan
        rows = length // chan
        index = lax.axis_index("chan")
        plane = lax.axis_index("space")
        group, core = index // CORES, index % CORES
        place = jnp.stack([group, core, plane, jnp.int32(space), jnp.int32(chan)]).astype(jnp.int32)

        own_one, beside_one = arranged(weight_one)
        own_two, beside_two = arranged(weight_two)

        tall = CORES * rows + 2 * RIM
        pieces = call(
            pack_kernel,
            [jax.ShapeDtypeStruct((1, tall, width, lanes), BF16)] * groups,
            [place, volume],
            [pltpu.VMEM((length + 2 * RIM, width, lanes), BF16)],
            name="pack_rows",
        )
        kept = jnp.zeros((groups, tall, width, lanes), BF16)
        kept = lax.dynamic_update_slice_in_dim(kept, pieces[0], group, 0)
        for k in range(1, groups):
            got = lax.ppermute(pieces[k], "chan", ahead(k))
            kept = lax.dynamic_update_slice_in_dim(kept, got, (group + groups - k) % groups, 0)

        def from_other_core(array, core):
            sent = lax.dynamic_slice_in_dim(array, (1 - core) * rows, rows + 2 * RIM, 1)
            return lax.ppermute(sent, "chan", swap)

        before = lax.ppermute(kept, "space", up)
        after = lax.ppermute(kept, "space", down)
        joined = (rows + 2 * RIM, full, lanes)
        own, done = call(
            first_own_kernel,
            [jax.ShapeDtypeStruct((rows + RIM, full, lanes), F32), jax.ShapeDtypeStruct((1,), jnp.int32)],
            [place, kept, from_other_core(kept, core), own_one, beside_one, bias_one[:, None]],
            [pltpu.VMEM(joined, BF16)],
            cost_estimate=cost(rows + RIM, 1, full, lanes),
            name="first_own",
        )
        hidden = call(
            first_kernel,
            jax.ShapeDtypeStruct((rows + RIM, full, lanes), BF16),
            [place, before, from_other_core(before, done[0]), after, from_other_core(after, done[0]), own, beside_one, bias_one[:, None]],
            [pltpu.VMEM((2, *joined), BF16)],
            cost_estimate=cost(rows + RIM, 2, full, lanes),
            name="first_layer",
        )

        before = lax.ppermute(hidden, "space", up)
        after = lax.ppermute(hidden, "space", down)
        own = call(
            second_own_kernel,
            jax.ShapeDtypeStruct((rows, full, lanes), F32),
            [hidden, own_two],
            cost_estimate=cost(rows, 1, full, lanes),
            name="second_own",
        )
        blocks = call(
            second_kernel,
            [jax.ShapeDtypeStruct((CORES, rows, width, lanes), BF16)] * groups,
            [place, before, after, own, beside_two, bias_two[:, None]],
            [pltpu.VMEM((groups, CORES, rows, width, lanes), BF16)],
            cost_estimate=cost(rows, 2, full, lanes),
            name="second_layer",
        )

        blocks = [blocks[0]] + [lax.ppermute(blocks[k], "chan", ahead(k)) for k in range(1, groups)]
        theirs = jnp.stack([lax.dynamic_index_in_dim(b, 1 - core, 0, keepdims=False) for b in blocks])
        swapped = lax.ppermute(theirs, "chan", swap)
        return call(
            unpack_kernel,
            jax.ShapeDtypeStruct(volume.shape, BF16),
            [place, swapped, *blocks],
            [pltpu.VMEM((chan, rows, width, lanes), BF16)],
            name="unpack_rows",
        )

    placed = (P("chan", "space", None, None), P(), P(), P(), P())
    return jax.shard_map(
        per_device,
        mesh=mesh,
        in_specs=placed,
        out_specs=P("chan", "space", None, None),
        check_vma=False,
    )
```

```python
import jax
import jax.numpy as jnp
from jax import lax
from jax.experimental import pallas as pl
from jax.experimental.pallas import tpu as pltpu
from jax.sharding import PartitionSpec as P

BF16 = jnp.bfloat16
F32 = jnp.float32
CORES = 2
RIM = 2
PARAMS = pltpu.CompilerParams(vmem_limit_bytes=24 * 1024 * 1024)
VMEM = pl.BlockSpec(memory_space=pltpu.VMEM)
SMEM = pl.BlockSpec(memory_space=pltpu.SMEM)


def along_lanes(total, lanes):
    chans = total.shape[0] // 3
    lane = lax.broadcasted_iota(jnp.int32, (chans, lanes), 1)
    low = pltpu.roll(total[:chans], 1, 1)
    high = pltpu.roll(total[2 * chans :], lanes - 1, 1)
    return (
        total[chans : 2 * chans]
        + jnp.where(lane == 0, 0.0, low)
        + jnp.where(lane == lanes - 1, 0.0, high)
    )


def conv_rows(get, planes, weight, store, rows, lanes):
    for start in range(0, rows, 2):
        parts = []
        for a in range(planes):
            for e in range(3):
                pair = [get(a, start + e + n) for n in range(2)]
                parts.append(jnp.concatenate(pair, axis=1))
        stacked = jnp.concatenate(parts, axis=0)
        total = jnp.dot(weight, stacked, preferred_element_type=F32)
        for n in range(2):
            store(start + n, along_lanes(total[:, n * lanes : (n + 1) * lanes], lanes))


def pack_kernel(place_ref, volume_ref, *refs):
    outs, rows_ref = refs[:-1], refs[-1]
    width, _, length, lanes = volume_ref.shape
    groups = len(outs)
    rows = length // groups
    edge = jnp.zeros((RIM, width, lanes), BF16)
    rows_ref[:RIM] = edge
    rows_ref[RIM + length :] = edge
    turned = jnp.swapaxes(volume_ref[:, 0].astype(F32), 0, 1)
    rows_ref[RIM : RIM + length] = turned.astype(BF16)
    for k in range(groups):
        target = lax.rem(place_ref[0] + k, groups)
        outs[k][0] = rows_ref[pl.ds(target * rows, rows + 2 * RIM)]


def own_kernel(own_ref, weight_ref, out_ref):
    rows, _, lanes = out_ref.shape

    def get(_, row):
        if len(own_ref.shape) == 3:
            return own_ref[row]
        return jnp.concatenate([own_ref[g, row] for g in range(own_ref.shape[0])], axis=0)

    def store(row, value):
        out_ref[row] = value

    conv_rows(get, 1, weight_ref[...], store, rows, lanes)


def reader(place_ref, before_ref, after_ref):
    outside = (place_ref[2] == 0, place_ref[2] == place_ref[3] - 1)
    refs = (before_ref, after_ref)

    def get(a, row):
        ref = refs[a]
        if len(ref.shape) == 3:
            value = ref[row]
        else:
            value = jnp.concatenate([ref[g, row] for g in range(ref.shape[0])], axis=0)
        return jnp.where(outside[a], jnp.zeros_like(value), value)

    return get


def first_kernel(place_ref, before_ref, after_ref, own_ref, weight_ref, bias_ref, out_ref):
    rows, _, lanes = out_ref.shape
    group, core = place_ref[0], place_ref[1]
    block = group * CORES + core
    bias = bias_ref[...]

    def store(row, value):
        value = jnp.maximum(value + own_ref[row] + bias, 0.0)
        if row == 0:
            value = jnp.where(block == 0, 0.0, value)
        if row == rows - 1:
            value = jnp.where(block == place_ref[4] - 1, 0.0, value)
        out_ref[row] = value.astype(BF16)

    get = reader(place_ref, before_ref, after_ref)
    conv_rows(get, 2, weight_ref[...], store, rows, lanes)


def second_kernel(place_ref, before_ref, after_ref, own_ref, weight_ref, bias_ref, *refs):
    outs, all_ref = refs[:-1], refs[-1]
    groups, cores, rows, width, lanes = all_ref.shape
    bias = bias_ref[...]

    def store(row, value):
        value = jnp.maximum(value + own_ref[row] + bias, 0.0).astype(BF16)
        for g in range(groups):
            for c in range(cores):
                at = (g * cores + c) * width
                all_ref[g, c, row] = value[at : at + width]

    get = reader(place_ref, before_ref, after_ref)
    conv_rows(get, 2, weight_ref[...], store, rows, lanes)
    for k in range(groups):
        outs[k][...] = all_ref[lax.rem(place_ref[0] + k, groups)]


def unpack_kernel(place_ref, swapped_ref, *refs):
    blocks, out_ref, rows_ref = refs[:-2], refs[-2], refs[-1]
    groups = len(blocks)
    _, rows, width, lanes = blocks[0].shape
    group, core = place_ref[0], place_ref[1]
    for k in range(groups):
        source = lax.rem(group + groups - k, groups) * CORES
        rows_ref[source + core] = blocks[k][core]
        rows_ref[source + 1 - core] = swapped_ref[k]
    length = groups * CORES * rows
    turned = rows_ref[...].reshape(length, width, lanes).astype(F32)
    out_ref[:, 0] = jnp.swapaxes(turned, 0, 1).astype(BF16)


def arranged(weight):
    _, inner, outer = weight.shape
    taps = weight.reshape(3, 3, 3, inner, outer)
    own = taps[1].transpose(1, 3, 0, 2).reshape(3 * outer, 3 * inner)
    beside = taps[::2].transpose(2, 4, 0, 1, 3).reshape(3 * outer, 6 * inner)
    return own, beside


def cost(rows, planes, full, lanes):
    flops = 2 * rows * lanes * full * full * 9 * planes
    return pl.CostEstimate(flops=flops, bytes_accessed=4_000_000, transcendentals=0)


def solution(mesh):
    space = mesh.shape["space"]
    chan = mesh.shape["chan"]
    groups = chan // CORES
    swap = [(i, i ^ 1) for i in range(chan)]

    half = space // 2
    moved = {half - 1: space - 1, space - 1: half - 1}
    spot = [moved.get(i, i) for i in range(space)]
    up = [(spot[i], spot[(i + 1) % space]) for i in range(space)]
    down = [(j, i) for i, j in up]

    def ahead(k):
        return [
            (i * chan + j, spot[i] * chan + (j + CORES * k) % chan) for i in range(space) for j in range(chan)
        ]

    def call(kernel, shapes, inputs, scratch=(), **kwargs):
        single = not isinstance(shapes, list)
        return pl.pallas_call(
            kernel,
            out_shape=shapes,
            in_specs=[SMEM if x.ndim == 1 else VMEM for x in inputs],
            out_specs=VMEM if single else [VMEM] * len(shapes),
            scratch_shapes=scratch,
            compiler_params=PARAMS,
            **kwargs,
        )(*inputs)

    def per_device(volume, weight_one, bias_one, weight_two, bias_two):
        width, _, length, lanes = volume.shape
        full = width * chan
        rows = length // chan
        index = lax.axis_index("chan")
        spot_index = lax.axis_index("space")
        plane = jnp.where(spot_index == half - 1, space - 1, jnp.where(spot_index == space - 1, half - 1, spot_index))
        group, core = index // CORES, index % CORES
        place = jnp.stack([group, core, plane, jnp.int32(space), jnp.int32(chan)]).astype(jnp.int32)

        own_one, beside_one = arranged(weight_one)
        own_two, beside_two = arranged(weight_two)

        tall = CORES * rows + 2 * RIM
        pieces = call(
            pack_kernel,
            [jax.ShapeDtypeStruct((1, tall, width, lanes), BF16)] * groups,
            [place, volume],
            [pltpu.VMEM((length + 2 * RIM, width, lanes), BF16)],
            name="pack_rows",
        )
        kept = jnp.zeros((groups, tall, width, lanes), BF16)
        for k in range(groups):
            got = lax.ppermute(pieces[k], ("space", "chan"), ahead(k))
            kept = lax.dynamic_update_slice_in_dim(kept, got, (group + groups - k) % groups, 0)

        mine = lax.dynamic_slice_in_dim(kept, core * rows, rows + 2 * RIM, 1)
        theirs = lax.dynamic_slice_in_dim(kept, (1 - core) * rows, rows + 2 * RIM, 1)
        swapped = lax.ppermute(theirs, "chan", swap)
        first = jnp.where(core == 0, mine, swapped)
        second = jnp.where(core == 0, swapped, mine)
        whole = jnp.concatenate([first, second], axis=2)

        before = lax.ppermute(whole, "space", up)
        after = lax.ppermute(whole, "space", down)
        own = call(
            own_kernel,
            jax.ShapeDtypeStruct((rows + RIM, full, lanes), F32),
            [whole, own_one],
            cost_estimate=cost(rows + RIM, 1, full, lanes),
            name="first_own",
        )
        hidden = call(
            first_kernel,
            jax.ShapeDtypeStruct((rows + RIM, full, lanes), BF16),
            [place, before, after, own, beside_one, bias_one[:, None]],
            cost_estimate=cost(rows + RIM, 2, full, lanes),
            name="first_layer",
        )

        before = lax.ppermute(hidden, "space", up)
        after = lax.ppermute(hidden, "space", down)
        own = call(
            own_kernel,
            jax.ShapeDtypeStruct((rows, full, lanes), F32),
            [hidden, own_two],
            cost_estimate=cost(rows, 1, full, lanes),
            name="second_own",
        )
        blocks = call(
            second_kernel,
            [jax.ShapeDtypeStruct((CORES, rows, width, lanes), BF16)] * groups,
            [place, before, after, own, beside_two, bias_two[:, None]],
            [pltpu.VMEM((groups, CORES, rows, width, lanes), BF16)],
            cost_estimate=cost(rows, 2, full, lanes),
            name="second_layer",
        )

        blocks = [lax.ppermute(blocks[k], ("space", "chan"), ahead(k)) for k in range(groups)]
        theirs = jnp.stack([lax.dynamic_index_in_dim(b, 1 - core, 0, keepdims=False) for b in blocks])
        swapped = lax.ppermute(theirs, "chan", swap)
        return call(
            unpack_kernel,
            jax.ShapeDtypeStruct(volume.shape, BF16),
            [place, swapped, *blocks],
            [pltpu.VMEM((chan, rows, width, lanes), BF16)],
            name="unpack_rows",
        )

    placed = (P("chan", "space", None, None), P(), P(), P(), P())
    return jax.shard_map(
        per_device,
        mesh=mesh,
        in_specs=placed,
        out_specs=P("chan", "space", None, None),
        check_vma=False,
    )
```

```python
import jax
import jax.numpy as jnp
from jax import lax
from jax.experimental import pallas as pl
from jax.experimental.pallas import tpu as pltpu
from jax.sharding import PartitionSpec as P

BF16 = jnp.bfloat16
F32 = jnp.float32
CORES = 2
RIM = 2
PARAMS = pltpu.CompilerParams(vmem_limit_bytes=24 * 1024 * 1024)
VMEM = pl.BlockSpec(memory_space=pltpu.VMEM)
SMEM = pl.BlockSpec(memory_space=pltpu.SMEM)


def along_lanes(total, lanes):
    chans = total.shape[0] // 3
    lane = lax.broadcasted_iota(jnp.int32, (chans, lanes), 1)
    low = pltpu.roll(total[:chans], 1, 1)
    high = pltpu.roll(total[2 * chans :], lanes - 1, 1)
    return (
        total[chans : 2 * chans]
        + jnp.where(lane == 0, 0.0, low)
        + jnp.where(lane == lanes - 1, 0.0, high)
    )


def conv_rows(get, planes, weight, store, rows, lanes):
    for start in range(0, rows, 2):
        parts = []
        for a in range(planes):
            for e in range(3):
                pair = [get(a, start + e + n) for n in range(2)]
                parts.append(jnp.concatenate(pair, axis=1))
        stacked = jnp.concatenate(parts, axis=0)
        total = jnp.dot(weight, stacked, preferred_element_type=F32)
        for n in range(2):
            store(start + n, along_lanes(total[:, n * lanes : (n + 1) * lanes], lanes))


def pack_kernel(place_ref, volume_ref, *refs):
    outs, rows_ref = refs[:-1], refs[-1]
    width, _, length, lanes = volume_ref.shape
    groups = len(outs)
    rows = length // groups
    edge = jnp.zeros((RIM, width, lanes), BF16)
    rows_ref[:RIM] = edge
    rows_ref[RIM + length :] = edge
    turned = jnp.swapaxes(volume_ref[:, 0].astype(F32), 0, 1)
    rows_ref[RIM : RIM + length] = turned.astype(BF16)
    for k in range(groups):
        target = lax.rem(place_ref[0] + k, groups)
        outs[k][0] = rows_ref[pl.ds(target * rows, rows + 2 * RIM)]


def rows_of(place_ref, ref, masked):
    def get(_, row):
        if len(ref.shape) == 3:
            value = ref[row]
        else:
            value = jnp.concatenate([ref[g, row] for g in range(ref.shape[0])], axis=0)
        if masked:
            value = jnp.where(place_ref[3] == 1, jnp.zeros_like(value), value)
        return value

    return get


def own_kernel(place_ref, plane_ref, weight_ref, out_ref):
    rows, _, lanes = out_ref.shape

    def store(row, value):
        out_ref[row] = value

    conv_rows(rows_of(place_ref, plane_ref, False), 1, weight_ref[...], store, rows, lanes)


def near_kernel(place_ref, plane_ref, weight_ref, before_ref, out_ref):
    rows, _, lanes = out_ref.shape

    def store(row, value):
        out_ref[row] = before_ref[row] + value

    weight = weight_ref[1 - place_ref[2]]
    conv_rows(rows_of(place_ref, plane_ref, False), 1, weight, store, rows, lanes)


def first_kernel(place_ref, plane_ref, weight_ref, before_ref, bias_ref, out_ref):
    rows, _, lanes = out_ref.shape
    block = place_ref[0] * CORES + place_ref[1]
    bias = bias_ref[...]

    def store(row, value):
        value = jnp.maximum(value + before_ref[row] + bias, 0.0)
        if row == 0:
            value = jnp.where(block == 0, 0.0, value)
        if row == rows - 1:
            value = jnp.where(block == place_ref[4] - 1, 0.0, value)
        out_ref[row] = value.astype(BF16)

    weight = weight_ref[place_ref[2]]
    conv_rows(rows_of(place_ref, plane_ref, True), 1, weight, store, rows, lanes)


def second_kernel(place_ref, plane_ref, weight_ref, before_ref, bias_ref, *refs):
    outs, all_ref = refs[:-1], refs[-1]
    groups, cores, rows, width, lanes = all_ref.shape
    bias = bias_ref[...]

    def store(row, value):
        value = jnp.maximum(value + before_ref[row] + bias, 0.0).astype(BF16)
        for g in range(groups):
            for c in range(cores):
                at = (g * cores + c) * width
                all_ref[g, c, row] = value[at : at + width]

    weight = weight_ref[place_ref[2]]
    conv_rows(rows_of(place_ref, plane_ref, True), 1, weight, store, rows, lanes)
    for k in range(groups):
        outs[k][...] = all_ref[lax.rem(place_ref[0] + k, groups)]


def unpack_kernel(place_ref, swapped_ref, *refs):
    blocks, out_ref, rows_ref = refs[:-2], refs[-2], refs[-1]
    groups = len(blocks)
    _, rows, width, lanes = blocks[0].shape
    group, core = place_ref[0], place_ref[1]
    for k in range(groups):
        source = lax.rem(group + groups - k, groups) * CORES
        rows_ref[source + core] = blocks[k][core]
        rows_ref[source + 1 - core] = swapped_ref[k]
    length = groups * CORES * rows
    turned = rows_ref[...].reshape(length, width, lanes).astype(F32)
    out_ref[:, 0] = jnp.swapaxes(turned, 0, 1).astype(BF16)


def arranged(weight):
    _, inner, outer = weight.shape
    taps = weight.reshape(3, 3, 3, inner, outer)
    own = taps[1].transpose(1, 3, 0, 2).reshape(3 * outer, 3 * inner)
    beside = taps[::2].transpose(0, 2, 4, 1, 3).reshape(2, 3 * outer, 3 * inner)
    return own, beside


def cost(rows, planes, full, lanes):
    flops = 2 * rows * lanes * full * full * 9 * planes
    return pl.CostEstimate(flops=flops, bytes_accessed=4_000_000, transcendentals=0)


def solution(mesh):
    space = mesh.shape["space"]
    chan = mesh.shape["chan"]
    groups = chan // CORES
    swap = [(i, i ^ 1) for i in range(chan)]

    near = [(i, i ^ 1) for i in range(space)]

    def far_partner(i, j):
        if i in (0, space - 1):
            return i * chan + (j ^ 1)
        return (((i - 1) ^ 1) + 1) * chan + j

    far = [(i * chan + j, far_partner(i, j)) for i in range(space) for j in range(chan)]

    def ahead(k):
        return [(i, (i + CORES * k) % chan) for i in range(chan)]

    def call(kernel, shapes, inputs, scratch=(), **kwargs):
        single = not isinstance(shapes, list)
        return pl.pallas_call(
            kernel,
            out_shape=shapes,
            in_specs=[SMEM if x.ndim == 1 else VMEM for x in inputs],
            out_specs=VMEM if single else [VMEM] * len(shapes),
            scratch_shapes=scratch,
            compiler_params=PARAMS,
            **kwargs,
        )(*inputs)

    def per_device(volume, weight_one, bias_one, weight_two, bias_two):
        width, _, length, lanes = volume.shape
        full = width * chan
        rows = length // chan
        index = lax.axis_index("chan")
        plane = lax.axis_index("space")
        edge = (plane == 0) | (plane == space - 1)
        group, core = index // CORES, index % CORES
        place = jnp.stack([group, core, plane % 2, edge.astype(jnp.int32), jnp.int32(chan)]).astype(jnp.int32)

        own_one, beside_one = arranged(weight_one)
        own_two, beside_two = arranged(weight_two)

        tall = CORES * rows + 2 * RIM
        pieces = call(
            pack_kernel,
            [jax.ShapeDtypeStruct((1, tall, width, lanes), BF16)] * groups,
            [place, volume],
            [pltpu.VMEM((length + 2 * RIM, width, lanes), BF16)],
            name="pack_rows",
        )
        kept = jnp.zeros((groups, tall, width, lanes), BF16)
        kept = lax.dynamic_update_slice_in_dim(kept, pieces[0], group, 0)
        for k in range(1, groups):
            got = lax.ppermute(pieces[k], "chan", ahead(k))
            kept = lax.dynamic_update_slice_in_dim(kept, got, (group + groups - k) % groups, 0)

        mine = lax.dynamic_slice_in_dim(kept, core * rows, rows + 2 * RIM, 1)
        theirs = lax.dynamic_slice_in_dim(kept, (1 - core) * rows, rows + 2 * RIM, 1)
        swapped = lax.ppermute(theirs, "chan", swap)
        first = jnp.where(core == 0, mine, swapped)
        second = jnp.where(core == 0, swapped, mine)
        whole = jnp.concatenate([first, second], axis=2)

        def layer(array, name, own_weight, beside_weight, bias, height, kernel, shapes, scratch=()):
            far_plane = lax.ppermute(array, ("space", "chan"), far)
            near_plane = lax.ppermute(array, "space", near)
            partial = jax.ShapeDtypeStruct((height, full, lanes), F32)
            work = cost(height, 1, full, lanes)
            total = call(own_kernel, partial, [place, array, own_weight], cost_estimate=work, name=name + "_own")
            total = call(
                near_kernel,
                partial,
                [place, near_plane, beside_weight, total],
                cost_estimate=work,
                name=name + "_near",
            )
            return call(
                kernel,
                shapes,
                [place, far_plane, beside_weight, total, bias[:, None]],
                scratch,
                cost_estimate=work,
                name=name + "_far",
            )

        hidden = layer(
            whole,
            "first",
            own_one,
            beside_one,
            bias_one,
            rows + RIM,
            first_kernel,
            jax.ShapeDtypeStruct((rows + RIM, full, lanes), BF16),
        )
        blocks = layer(
            hidden,
            "second",
            own_two,
            beside_two,
            bias_two,
            rows,
            second_kernel,
            [jax.ShapeDtypeStruct((CORES, rows, width, lanes), BF16)] * groups,
            [pltpu.VMEM((groups, CORES, rows, width, lanes), BF16)],
        )

        blocks = [blocks[0]] + [lax.ppermute(blocks[k], "chan", ahead(k)) for k in range(1, groups)]
        theirs = jnp.stack([lax.dynamic_index_in_dim(b, 1 - core, 0, keepdims=False) for b in blocks])
        swapped = lax.ppermute(theirs, "chan", swap)
        return call(
            unpack_kernel,
            jax.ShapeDtypeStruct(volume.shape, BF16),
            [place, swapped, *blocks],
            [pltpu.VMEM((chan, rows, width, lanes), BF16)],
            name="unpack_rows",
        )

    placed = (P("chan", "space", None, None), P(), P(), P(), P())
    return jax.shard_map(
        per_device,
        mesh=mesh,
        in_specs=placed,
        out_specs=P("chan", "space", None, None),
        check_vma=False,
    )
```

```python
import jax
import jax.numpy as jnp
from jax import lax
from jax.experimental import pallas as pl
from jax.experimental.pallas import tpu as pltpu
from jax.sharding import PartitionSpec as P

BF16 = jnp.bfloat16
F32 = jnp.float32
CORES = 2
RIM = 2
PARAMS = pltpu.CompilerParams(vmem_limit_bytes=24 * 1024 * 1024)
VMEM = pl.BlockSpec(memory_space=pltpu.VMEM)


def my_group():
    return lax.axis_index("chan") // CORES


def my_core():
    return lax.axis_index("chan") % CORES


def along_lanes(total, lanes):
    chans = total.shape[0] // 3
    lane = lax.broadcasted_iota(jnp.int32, (chans, lanes), 1)
    low = pltpu.roll(total[:chans], 1, 1)
    high = pltpu.roll(total[2 * chans :], lanes - 1, 1)
    return (
        total[chans : 2 * chans]
        + jnp.where(lane == 0, 0.0, low)
        + jnp.where(lane == lanes - 1, 0.0, high)
    )


def conv_rows(get, planes, weight, store, rows, lanes):
    for start in range(0, rows, 2):
        parts = []
        for a in range(planes):
            for e in range(3):
                pair = [get(a, start + e + n) for n in range(2)]
                parts.append(jnp.concatenate(pair, axis=1))
        stacked = jnp.concatenate(parts, axis=0)
        total = jnp.dot(weight, stacked, preferred_element_type=F32)
        for n in range(2):
            store(start + n, along_lanes(total[:, n * lanes : (n + 1) * lanes], lanes))


def pack_kernel(volume_ref, *refs):
    outs, rows_ref = refs[:-1], refs[-1]
    width, _, length, lanes = volume_ref.shape
    groups = len(outs)
    rows = length // groups
    edge = jnp.zeros((RIM, width, lanes), BF16)
    rows_ref[:RIM] = edge
    rows_ref[RIM + length :] = edge
    turned = jnp.swapaxes(volume_ref[:, 0].astype(F32), 0, 1)
    rows_ref[RIM : RIM + length] = turned.astype(BF16)
    for k in range(groups):
        target = lax.rem(my_group() + k, groups)
        outs[k][0] = rows_ref[pl.ds(target * rows, rows + 2 * RIM)]


def rows_of(ref, masked):
    def get(_, row):
        if len(ref.shape) == 3:
            value = ref[row]
        else:
            value = jnp.concatenate([ref[g, row] for g in range(ref.shape[0])], axis=0)
        if masked:
            plane = lax.axis_index("space")
            edge = (plane == 0) | (plane == lax.axis_size("space") - 1)
            value = jnp.where(edge, jnp.zeros_like(value), value)
        return value

    return get


def own_kernel(plane_ref, weight_ref, out_ref):
    rows, _, lanes = out_ref.shape

    def store(row, value):
        out_ref[row] = value

    conv_rows(rows_of(plane_ref, False), 1, weight_ref[...], store, rows, lanes)


def near_kernel(plane_ref, weight_ref, before_ref, out_ref):
    rows, _, lanes = out_ref.shape

    def store(row, value):
        out_ref[row] = before_ref[row] + value

    weight = weight_ref[1 - lax.axis_index("space") % 2]
    conv_rows(rows_of(plane_ref, False), 1, weight, store, rows, lanes)


def first_kernel(plane_ref, weight_ref, before_ref, bias_ref, out_ref):
    rows, _, lanes = out_ref.shape
    block = lax.axis_index("chan")
    bias = bias_ref[...]

    def store(row, value):
        value = jnp.maximum(value + before_ref[row] + bias, 0.0)
        if row == 0:
            value = jnp.where(block == 0, 0.0, value)
        if row == rows - 1:
            value = jnp.where(block == lax.axis_size("chan") - 1, 0.0, value)
        out_ref[row] = value.astype(BF16)

    weight = weight_ref[lax.axis_index("space") % 2]
    conv_rows(rows_of(plane_ref, True), 1, weight, store, rows, lanes)


def second_kernel(plane_ref, weight_ref, before_ref, bias_ref, *refs):
    outs, all_ref = refs[:-1], refs[-1]
    groups, cores, rows, width, lanes = all_ref.shape
    bias = bias_ref[...]

    def store(row, value):
        value = jnp.maximum(value + before_ref[row] + bias, 0.0).astype(BF16)
        for g in range(groups):
            for c in range(cores):
                at = (g * cores + c) * width
                all_ref[g, c, row] = value[at : at + width]

    weight = weight_ref[lax.axis_index("space") % 2]
    conv_rows(rows_of(plane_ref, True), 1, weight, store, rows, lanes)
    for k in range(groups):
        outs[k][...] = all_ref[lax.rem(my_group() + k, groups)]


def unpack_kernel(swapped_ref, *refs):
    blocks, out_ref, rows_ref = refs[:-2], refs[-2], refs[-1]
    groups = len(blocks)
    _, rows, width, lanes = blocks[0].shape
    group, core = my_group(), my_core()
    for k in range(groups):
        source = lax.rem(group + groups - k, groups) * CORES
        rows_ref[source + core] = blocks[k][core]
        rows_ref[source + 1 - core] = swapped_ref[k]
    length = groups * CORES * rows
    turned = rows_ref[...].reshape(length, width, lanes).astype(F32)
    out_ref[:, 0] = jnp.swapaxes(turned, 0, 1).astype(BF16)


def arranged(weight):
    _, inner, outer = weight.shape
    taps = weight.reshape(3, 3, 3, inner, outer)
    own = taps[1].transpose(1, 3, 0, 2).reshape(3 * outer, 3 * inner)
    beside = taps[::2].transpose(0, 2, 4, 1, 3).reshape(2, 3 * outer, 3 * inner)
    return own, beside


def cost(rows, planes, full, lanes):
    flops = 2 * rows * lanes * full * full * 9 * planes
    return pl.CostEstimate(flops=flops, bytes_accessed=4_000_000, transcendentals=0)


def solution(mesh):
    space = mesh.shape["space"]
    chan = mesh.shape["chan"]
    groups = chan // CORES
    swap = [(i, i ^ 1) for i in range(chan)]

    near = [(i, i ^ 1) for i in range(space)]

    def far_partner(i, j):
        if i in (0, space - 1):
            return i * chan + (j ^ 1)
        return (((i - 1) ^ 1) + 1) * chan + j

    far = [(i * chan + j, far_partner(i, j)) for i in range(space) for j in range(chan)]

    def ahead(k):
        return [(i, (i + CORES * k) % chan) for i in range(chan)]

    def call(kernel, shapes, inputs, scratch=(), **kwargs):
        single = not isinstance(shapes, list)
        return pl.pallas_call(
            kernel,
            out_shape=shapes,
            in_specs=[VMEM] * len(inputs),
            out_specs=VMEM if single else [VMEM] * len(shapes),
            scratch_shapes=scratch,
            compiler_params=PARAMS,
            **kwargs,
        )(*inputs)

    def per_device(volume, weight_one, bias_one, weight_two, bias_two):
        width, _, length, lanes = volume.shape
        full = width * chan
        rows = length // chan
        index = lax.axis_index("chan")
        group, core = index // CORES, index % CORES

        own_one, beside_one = arranged(weight_one)
        own_two, beside_two = arranged(weight_two)

        tall = CORES * rows + 2 * RIM
        pieces = call(
            pack_kernel,
            [jax.ShapeDtypeStruct((1, tall, width, lanes), BF16)] * groups,
            [volume],
            [pltpu.VMEM((length + 2 * RIM, width, lanes), BF16)],
            name="pack_rows",
        )
        kept = jnp.zeros((groups, tall, width, lanes), BF16)
        kept = lax.dynamic_update_slice_in_dim(kept, pieces[0], group, 0)
        for k in range(1, groups):
            got = lax.ppermute(pieces[k], "chan", ahead(k))
            kept = lax.dynamic_update_slice_in_dim(kept, got, (group + groups - k) % groups, 0)

        mine = lax.dynamic_slice_in_dim(kept, core * rows, rows + 2 * RIM, 1)
        theirs = lax.dynamic_slice_in_dim(kept, (1 - core) * rows, rows + 2 * RIM, 1)
        swapped = lax.ppermute(theirs, "chan", swap)
        first = jnp.where(core == 0, mine, swapped)
        second = jnp.where(core == 0, swapped, mine)
        whole = jnp.concatenate([first, second], axis=2)

        def layer(array, name, own_weight, beside_weight, bias, height, kernel, shapes, scratch=()):
            far_plane = lax.ppermute(array, ("space", "chan"), far)
            near_plane = lax.ppermute(array, "space", near)
            partial = jax.ShapeDtypeStruct((height, full, lanes), F32)
            work = cost(height, 1, full, lanes)
            total = call(own_kernel, partial, [array, own_weight], cost_estimate=work, name=name + "_own")
            total = call(
                near_kernel,
                partial,
                [near_plane, beside_weight, total],
                cost_estimate=work,
                name=name + "_near",
            )
            return call(
                kernel,
                shapes,
                [far_plane, beside_weight, total, bias[:, None]],
                scratch,
                cost_estimate=work,
                name=name + "_far",
            )

        hidden = layer(
            whole,
            "first",
            own_one,
            beside_one,
            bias_one,
            rows + RIM,
            first_kernel,
            jax.ShapeDtypeStruct((rows + RIM, full, lanes), BF16),
        )
        blocks = layer(
            hidden,
            "second",
            own_two,
            beside_two,
            bias_two,
            rows,
            second_kernel,
            [jax.ShapeDtypeStruct((CORES, rows, width, lanes), BF16)] * groups,
            [pltpu.VMEM((groups, CORES, rows, width, lanes), BF16)],
        )

        blocks = [blocks[0]] + [lax.ppermute(blocks[k], "chan", ahead(k)) for k in range(1, groups)]
        theirs = jnp.stack([lax.dynamic_index_in_dim(b, 1 - core, 0, keepdims=False) for b in blocks])
        swapped = lax.ppermute(theirs, "chan", swap)
        return call(
            unpack_kernel,
            jax.ShapeDtypeStruct(volume.shape, BF16),
            [swapped, *blocks],
            [pltpu.VMEM((chan, rows, width, lanes), BF16)],
            name="unpack_rows",
        )

    placed = (P("chan", "space", None, None), P(), P(), P(), P())
    return jax.shard_map(
        per_device,
        mesh=mesh,
        in_specs=placed,
        out_specs=P("chan", "space", None, None),
        check_vma=False,
    )
```

```python
import jax
import jax.numpy as jnp
from jax import lax
from jax.experimental import pallas as pl
from jax.experimental.pallas import tpu as pltpu
from jax.sharding import PartitionSpec as P

BF16 = jnp.bfloat16
F32 = jnp.float32
CORES = 2
RIM = 2
PARAMS = pltpu.CompilerParams(vmem_limit_bytes=24 * 1024 * 1024)
VMEM = pl.BlockSpec(memory_space=pltpu.VMEM)


def my_group():
    return lax.axis_index("chan") // CORES


def my_core():
    return lax.axis_index("chan") % CORES


def along_lanes(total, lanes):
    chans = total.shape[0] // 3
    lane = lax.broadcasted_iota(jnp.int32, (chans, lanes), 1)
    low = pltpu.roll(total[:chans], 1, 1)
    high = pltpu.roll(total[2 * chans :], lanes - 1, 1)
    return (
        total[chans : 2 * chans]
        + jnp.where(lane == 0, 0.0, low)
        + jnp.where(lane == lanes - 1, 0.0, high)
    )


def conv_rows(get, planes, weight, store, rows, lanes):
    for start in range(0, rows, 2):
        parts = []
        for a in range(planes):
            for e in range(3):
                pair = [get(a, start + e + n) for n in range(2)]
                parts.append(jnp.concatenate(pair, axis=1))
        stacked = jnp.concatenate(parts, axis=0)
        total = jnp.dot(weight, stacked, preferred_element_type=F32)
        for n in range(2):
            store(start + n, along_lanes(total[:, n * lanes : (n + 1) * lanes], lanes))


def pack_kernel(volume_ref, *refs):
    outs, rows_ref = refs[:-1], refs[-1]
    width, _, length, lanes = volume_ref.shape
    groups = len(outs)
    rows = length // groups
    edge = jnp.zeros((RIM, width, lanes), BF16)
    rows_ref[:RIM] = edge
    rows_ref[RIM + length :] = edge
    turned = jnp.swapaxes(volume_ref[:, 0].astype(F32), 0, 1)
    rows_ref[RIM : RIM + length] = turned.astype(BF16)
    for k in range(groups):
        target = lax.rem(my_group() + k, groups)
        outs[k][0] = rows_ref[pl.ds(target * rows, rows + 2 * RIM)]


def gather_rows(kept_ref, other_ref, joined_ref):
    core = my_core()
    groups, rows, width, lanes = other_ref.shape
    offset = core * (kept_ref.shape[1] - rows)
    for row in range(rows):
        parts = []
        for g in range(groups):
            kept = kept_ref[g, offset + row]
            other = other_ref[g, row]
            parts += [jnp.where(core == 0, kept, other), jnp.where(core == 0, other, kept)]
        joined_ref[row] = jnp.concatenate(parts, axis=0)


def rows_of(ref, masked):
    def get(_, row):
        value = ref[row]
        if masked:
            plane = lax.axis_index("space")
            edge = (plane == 0) | (plane == lax.axis_size("space") - 1)
            value = jnp.where(edge, jnp.zeros_like(value), value)
        return value

    return get


def own_kernel(plane_ref, weight_ref, out_ref):
    rows, _, lanes = out_ref.shape

    def store(row, value):
        out_ref[row] = value

    conv_rows(rows_of(plane_ref, False), 1, weight_ref[...], store, rows, lanes)


def near_kernel(plane_ref, weight_ref, before_ref, out_ref):
    rows, _, lanes = out_ref.shape

    def store(row, value):
        out_ref[row] = before_ref[row] + value

    weight = weight_ref[1 - lax.axis_index("space") % 2]
    conv_rows(rows_of(plane_ref, False), 1, weight, store, rows, lanes)


def first_own_kernel(kept_ref, other_ref, weight_ref, later_ref, bias_ref, out_ref, zero_ref, joined_ref):
    gather_rows(kept_ref, other_ref, joined_ref)
    own_kernel(joined_ref, weight_ref, out_ref)
    zero_ref[...] = jnp.zeros_like(zero_ref)


def first_near_kernel(kept_ref, other_ref, weight_ref, before_ref, out_ref, joined_ref):
    gather_rows(kept_ref, other_ref, joined_ref)
    near_kernel(joined_ref, weight_ref, before_ref, out_ref)


def first_far_kernel(kept_ref, other_ref, weight_ref, before_ref, bias_ref, out_ref, joined_ref):
    gather_rows(kept_ref, other_ref, joined_ref)
    rows, _, lanes = out_ref.shape
    block = lax.axis_index("chan")
    bias = bias_ref[...]

    def store(row, value):
        value = jnp.maximum(value + before_ref[row] + bias, 0.0)
        if row == 0:
            value = jnp.where(block == 0, 0.0, value)
        if row == rows - 1:
            value = jnp.where(block == lax.axis_size("chan") - 1, 0.0, value)
        out_ref[row] = value.astype(BF16)

    weight = weight_ref[lax.axis_index("space") % 2]
    conv_rows(rows_of(joined_ref, True), 1, weight, store, rows, lanes)


def second_kernel(plane_ref, weight_ref, before_ref, bias_ref, *refs):
    outs, all_ref = refs[:-1], refs[-1]
    groups, cores, rows, width, lanes = all_ref.shape
    bias = bias_ref[...]

    def store(row, value):
        value = jnp.maximum(value + before_ref[row] + bias, 0.0).astype(BF16)
        for g in range(groups):
            for c in range(cores):
                at = (g * cores + c) * width
                all_ref[g, c, row] = value[at : at + width]

    weight = weight_ref[lax.axis_index("space") % 2]
    conv_rows(rows_of(plane_ref, True), 1, weight, store, rows, lanes)
    for k in range(groups):
        outs[k][...] = all_ref[lax.rem(my_group() + k, groups)]


def unpack_kernel(swapped_ref, *refs):
    blocks, out_ref, rows_ref = refs[:-2], refs[-2], refs[-1]
    groups = len(blocks)
    _, rows, width, lanes = blocks[0].shape
    group, core = my_group(), my_core()
    for k in range(groups):
        source = lax.rem(group + groups - k, groups) * CORES
        rows_ref[source + core] = blocks[k][core]
        rows_ref[source + 1 - core] = swapped_ref[k]
    length = groups * CORES * rows
    turned = rows_ref[...].reshape(length, width, lanes).astype(F32)
    out_ref[:, 0] = jnp.swapaxes(turned, 0, 1).astype(BF16)


def arranged(weight):
    _, inner, outer = weight.shape
    taps = weight.reshape(3, 3, 3, inner, outer)
    own = taps[1].transpose(1, 3, 0, 2).reshape(3 * outer, 3 * inner)
    beside = taps[::2].transpose(0, 2, 4, 1, 3).reshape(2, 3 * outer, 3 * inner)
    return own, beside


def cost(rows, planes, full, lanes):
    flops = 2 * rows * lanes * full * full * 9 * planes
    return pl.CostEstimate(flops=flops, bytes_accessed=4_000_000, transcendentals=0)


def solution(mesh):
    space = mesh.shape["space"]
    chan = mesh.shape["chan"]
    groups = chan // CORES
    swap = [(i, i ^ 1) for i in range(chan)]

    near = [(i, i ^ 1) for i in range(space)]

    def far_partner(i, j):
        if i in (0, space - 1):
            return i * chan + (j ^ 1)
        return (((i - 1) ^ 1) + 1) * chan + j

    far = [(i * chan + j, far_partner(i, j)) for i in range(space) for j in range(chan)]

    def ahead(k):
        return [(i, (i + CORES * k) % chan) for i in range(chan)]

    def call(kernel, shapes, inputs, scratch=(), **kwargs):
        single = not isinstance(shapes, list)
        return pl.pallas_call(
            kernel,
            out_shape=shapes,
            in_specs=[VMEM] * len(inputs),
            out_specs=VMEM if single else [VMEM] * len(shapes),
            scratch_shapes=scratch,
            compiler_params=PARAMS,
            **kwargs,
        )(*inputs)

    def per_device(volume, weight_one, bias_one, weight_two, bias_two):
        width, _, length, lanes = volume.shape
        full = width * chan
        rows = length // chan
        index = lax.axis_index("chan")
        group, core = index // CORES, index % CORES

        own_one, beside_one = arranged(weight_one)
        own_two, beside_two = arranged(weight_two)

        tall = CORES * rows + 2 * RIM
        pieces = call(
            pack_kernel,
            [jax.ShapeDtypeStruct((1, tall, width, lanes), BF16)] * groups,
            [volume],
            [pltpu.VMEM((length + 2 * RIM, width, lanes), BF16)],
            name="pack_rows",
        )
        kept = jnp.zeros((groups, tall, width, lanes), BF16)
        kept = lax.dynamic_update_slice_in_dim(kept, pieces[0], group, 0)
        for k in range(1, groups):
            got = lax.ppermute(pieces[k], "chan", ahead(k))
            kept = lax.dynamic_update_slice_in_dim(kept, got, (group + groups - k) % groups, 0)

        def from_other_core(array, core):
            sent = lax.dynamic_slice_in_dim(array, (1 - core) * rows, rows + 2 * RIM, 1)
            return lax.ppermute(sent, "chan", swap)

        def halo(array):
            return lax.ppermute(array, ("space", "chan"), far), lax.ppermute(array, "space", near)

        partial = jax.ShapeDtypeStruct((rows + RIM, full, lanes), F32)
        joined = [pltpu.VMEM((rows + 2 * RIM, full, lanes), BF16)]
        work = cost(rows + RIM, 1, full, lanes)
        far_plane, near_plane = halo(kept)
        total, zero = call(
            first_own_kernel,
            [partial, jax.ShapeDtypeStruct((8, 128), jnp.int32)],
            [kept, from_other_core(kept, core), own_one, beside_one, bias_one[:, None]],
            joined,
            cost_estimate=work,
            name="first_own",
        )
        later_core = core + zero[0, 0]
        total = call(
            first_near_kernel,
            partial,
            [near_plane, from_other_core(near_plane, later_core), beside_one, total],
            joined,
            cost_estimate=work,
            name="first_near",
        )
        hidden = call(
            first_far_kernel,
            jax.ShapeDtypeStruct((rows + RIM, full, lanes), BF16),
            [far_plane, from_other_core(far_plane, later_core), beside_one, total, bias_one[:, None]],
            joined,
            cost_estimate=work,
            name="first_far",
        )

        partial = jax.ShapeDtypeStruct((rows, full, lanes), F32)
        work = cost(rows, 1, full, lanes)
        far_plane, near_plane = halo(hidden)
        total = call(own_kernel, partial, [hidden, own_two], cost_estimate=work, name="second_own")
        total = call(near_kernel, partial, [near_plane, beside_two, total], cost_estimate=work, name="second_near")
        blocks = call(
            second_kernel,
            [jax.ShapeDtypeStruct((CORES, rows, width, lanes), BF16)] * groups,
            [far_plane, beside_two, total, bias_two[:, None]],
            [pltpu.VMEM((groups, CORES, rows, width, lanes), BF16)],
            cost_estimate=work,
            name="second_far",
        )

        blocks = [blocks[0]] + [lax.ppermute(blocks[k], "chan", ahead(k)) for k in range(1, groups)]
        theirs = jnp.stack([lax.dynamic_index_in_dim(b, 1 - core, 0, keepdims=False) for b in blocks])
        swapped = lax.ppermute(theirs, "chan", swap)
        return call(
            unpack_kernel,
            jax.ShapeDtypeStruct(volume.shape, BF16),
            [swapped, *blocks],
            [pltpu.VMEM((chan, rows, width, lanes), BF16)],
            name="unpack_rows",
        )

    placed = (P("chan", "space", None, None), P(), P(), P(), P())
    return jax.shard_map(
        per_device,
        mesh=mesh,
        in_specs=placed,
        out_specs=P("chan", "space", None, None),
        check_vma=False,
    )
```

```python
import functools

import jax
import jax.numpy as jnp
from jax import lax
from jax.experimental import pallas as pl
from jax.experimental.pallas import tpu as pltpu
from jax.sharding import PartitionSpec as P

BF16 = jnp.bfloat16
F32 = jnp.float32
CORES = 2
RIM = 2
PARAMS = pltpu.CompilerParams(vmem_limit_bytes=24 * 1024 * 1024)
VMEM = pl.BlockSpec(memory_space=pltpu.VMEM)


def my_group():
    return lax.axis_index("chan") // CORES


def my_core():
    return lax.axis_index("chan") % CORES


def along_lanes(total, lanes):
    chans = total.shape[0] // 3
    lane = lax.broadcasted_iota(jnp.int32, (chans, lanes), 1)
    low = pltpu.roll(total[:chans], 1, 1)
    high = pltpu.roll(total[2 * chans :], lanes - 1, 1)
    return (
        total[chans : 2 * chans]
        + jnp.where(lane == 0, 0.0, low)
        + jnp.where(lane == lanes - 1, 0.0, high)
    )


def conv_rows(get, planes, weight, store, rows, lanes):
    for start in range(0, rows, 2):
        parts = []
        for a in range(planes):
            for e in range(3):
                pair = [get(a, start + e + n) for n in range(2)]
                parts.append(jnp.concatenate(pair, axis=1))
        stacked = jnp.concatenate(parts, axis=0)
        total = jnp.dot(weight, stacked, preferred_element_type=F32)
        for n in range(2):
            store(start + n, along_lanes(total[:, n * lanes : (n + 1) * lanes], lanes))


def pack_kernel(volume_ref, *refs):
    outs, rows_ref = refs[:-1], refs[-1]
    width, _, length, lanes = volume_ref.shape
    groups = len(outs)
    rows = length // groups
    edge = jnp.zeros((RIM, width, lanes), BF16)
    rows_ref[:RIM] = edge
    rows_ref[RIM + length :] = edge
    turned = jnp.swapaxes(volume_ref[:, 0].astype(F32), 0, 1)
    rows_ref[RIM : RIM + length] = turned.astype(BF16)
    for k in range(groups):
        target = lax.rem(my_group() + k, groups)
        outs[k][0] = rows_ref[pl.ds(target * rows, rows + 2 * RIM)]


def gather_rows(kept_ref, other_ref, joined_ref):
    core = my_core()
    groups, rows, width, lanes = other_ref.shape
    offset = core * (kept_ref.shape[1] - rows)
    for row in range(rows):
        parts = []
        for g in range(groups):
            kept = kept_ref[g, offset + row]
            other = other_ref[g, row]
            parts += [jnp.where(core == 0, kept, other), jnp.where(core == 0, other, kept)]
        joined_ref[row] = jnp.concatenate(parts, axis=0)


def rows_of(ref, masked):
    def get(_, row):
        value = ref[row]
        if masked:
            plane = lax.axis_index("space")
            edge = (plane == 0) | (plane == lax.axis_size("space") - 1)
            value = jnp.where(edge, jnp.zeros_like(value), value)
        return value

    return get


def own_kernel(plane_ref, weight_ref, out_ref):
    rows, _, lanes = out_ref.shape

    def store(row, value):
        out_ref[row] = value

    conv_rows(rows_of(plane_ref, False), 1, weight_ref[...], store, rows, lanes)


def near_kernel(plane_ref, weight_ref, before_ref, out_ref):
    rows, _, lanes = out_ref.shape

    def store(row, value):
        out_ref[row] = before_ref[row] + value

    weight = weight_ref[1 - lax.axis_index("space") % 2]
    conv_rows(rows_of(plane_ref, False), 1, weight, store, rows, lanes)


def ready_kernel(*refs):
    refs[-1][...] = jnp.zeros_like(refs[-1])


def first_own_kernel(kept_ref, other_ref, weight_ref, out_ref, zero_ref, joined_ref):
    gather_rows(kept_ref, other_ref, joined_ref)
    own_kernel(joined_ref, weight_ref, out_ref)
    zero_ref[...] = jnp.zeros_like(zero_ref)


def first_near_kernel(kept_ref, other_ref, weight_ref, before_ref, out_ref, joined_ref):
    gather_rows(kept_ref, other_ref, joined_ref)
    near_kernel(joined_ref, weight_ref, before_ref, out_ref)


def first_far_kernel(kept_ref, other_ref, weight_ref, before_ref, bias_ref, out_ref, joined_ref):
    gather_rows(kept_ref, other_ref, joined_ref)
    rows, _, lanes = out_ref.shape
    block = lax.axis_index("chan")
    bias = bias_ref[...]

    def store(row, value):
        value = jnp.maximum(value + before_ref[row] + bias, 0.0)
        if row == 0:
            value = jnp.where(block == 0, 0.0, value)
        if row == rows - 1:
            value = jnp.where(block == lax.axis_size("chan") - 1, 0.0, value)
        out_ref[row] = value.astype(BF16)

    weight = weight_ref[lax.axis_index("space") % 2]
    conv_rows(rows_of(joined_ref, True), 1, weight, store, rows, lanes)


def second_own_kernel(plane_ref, weight_ref, out_ref):
    rows, cores, _, lanes = out_ref.shape
    for c in range(cores):

        def store(row, value, c=c):
            out_ref[row, c] = value

        conv_rows(rows_of(plane_ref, False), 1, weight_ref[c], store, rows, lanes)


def second_near_kernel(plane_ref, weight_ref, before_ref, out_ref):
    rows, cores, _, lanes = out_ref.shape
    side = 1 - lax.axis_index("space") % 2
    for c in range(cores):

        def store(row, value, c=c):
            out_ref[row, c] = before_ref[row, c] + value

        conv_rows(rows_of(plane_ref, False), 1, weight_ref[side, c], store, rows, lanes)


def second_far_kernel(other, plane_ref, weight_ref, before_ref, bias_ref, *refs):
    outs, all_ref = refs[:-1], refs[-1]
    groups, rows, width, lanes = all_ref.shape
    c = 1 - my_core() if other else my_core()
    bias = bias_ref[c]

    def store(row, value):
        value = jnp.maximum(value + before_ref[row, c] + bias, 0.0).astype(BF16)
        for g in range(groups):
            all_ref[g, row] = value[g * width : (g + 1) * width]

    weight = weight_ref[lax.axis_index("space") % 2, c]
    conv_rows(rows_of(plane_ref, True), 1, weight, store, rows, lanes)
    for k in range(groups):
        target = lax.rem(my_group() + k, groups)
        if other:
            outs[0][k] = all_ref[target]
        else:
            outs[k][...] = all_ref[target]


def unpack_kernel(*refs):
    blocks, out_ref, rows_ref = refs[:-2], refs[-2], refs[-1]
    groups = len(blocks)
    _, rows, width, lanes = blocks[0].shape
    group, core = my_group(), my_core()
    for k in range(groups):
        source = lax.rem(group + groups - k, groups) * CORES
        rows_ref[source + core] = blocks[k][0]
        rows_ref[source + 1 - core] = blocks[k][1]
    length = groups * CORES * rows
    turned = rows_ref[...].reshape(length, width, lanes).astype(F32)
    out_ref[:, 0] = jnp.swapaxes(turned, 0, 1).astype(BF16)


def arranged(weight, width=None):
    _, inner, outer = weight.shape
    taps = weight.reshape(3, 3, 3, inner, outer).transpose(0, 2, 4, 1, 3)
    if width is None:
        taps = taps.reshape(3, 3 * outer, 3 * inner)
    else:
        taps = taps.reshape(3, 3, -1, CORES, width, 3 * inner).transpose(0, 3, 1, 2, 4, 5)
        taps = taps.reshape(3, CORES, 3 * outer // CORES, 3 * inner)
    return taps[1], taps[::2]


def cost(rows, planes, full, lanes):
    flops = 2 * rows * lanes * full * full * 9 * planes
    return pl.CostEstimate(flops=flops, bytes_accessed=4_000_000, transcendentals=0)


def solution(mesh):
    space = mesh.shape["space"]
    chan = mesh.shape["chan"]
    groups = chan // CORES
    swap = [(i, i ^ 1) for i in range(chan)]

    near = [(i, i ^ 1) for i in range(space)]

    def far_partner(i, j):
        if i in (0, space - 1):
            return i * chan + (j ^ 1)
        return (((i - 1) ^ 1) + 1) * chan + j

    far = [(i * chan + j, far_partner(i, j)) for i in range(space) for j in range(chan)]

    def ahead(k):
        return [(i, (i + CORES * k) % chan) for i in range(chan)]

    def call(kernel, shapes, inputs, scratch=(), **kwargs):
        single = not isinstance(shapes, list)
        return pl.pallas_call(
            kernel,
            out_shape=shapes,
            in_specs=[VMEM] * len(inputs),
            out_specs=VMEM if single else [VMEM] * len(shapes),
            scratch_shapes=scratch,
            compiler_params=PARAMS,
            **kwargs,
        )(*inputs)

    def per_device(volume, weight_one, bias_one, weight_two, bias_two):
        width, _, length, lanes = volume.shape
        full = width * chan
        rows = length // chan
        index = lax.axis_index("chan")
        group, core = index // CORES, index % CORES

        own_one, beside_one = arranged(weight_one)
        own_two, beside_two = arranged(weight_two, width)
        offsets_two = bias_two.reshape(groups, CORES, width).transpose(1, 0, 2).reshape(CORES, groups * width, 1)

        tall = CORES * rows + 2 * RIM
        pieces = call(
            pack_kernel,
            [jax.ShapeDtypeStruct((1, tall, width, lanes), BF16)] * groups,
            [volume],
            [pltpu.VMEM((length + 2 * RIM, width, lanes), BF16)],
            name="pack_rows",
        )
        kept = jnp.zeros((groups, tall, width, lanes), BF16)
        kept = lax.dynamic_update_slice_in_dim(kept, pieces[0], group, 0)
        for k in range(1, groups):
            got = lax.ppermute(pieces[k], "chan", ahead(k))
            kept = lax.dynamic_update_slice_in_dim(kept, got, (group + groups - k) % groups, 0)

        def from_other_core(array, core):
            sent = lax.dynamic_slice_in_dim(array, (1 - core) * rows, rows + 2 * RIM, 1)
            return lax.ppermute(sent, "chan", swap)

        def halo(array):
            return lax.ppermute(array, ("space", "chan"), far), lax.ppermute(array, "space", near)

        partial = jax.ShapeDtypeStruct((rows + RIM, full, lanes), F32)
        joined = [pltpu.VMEM((rows + 2 * RIM, full, lanes), BF16)]
        work = cost(rows + RIM, 1, full, lanes)
        far_plane, near_plane = halo(kept)
        zeros = jax.ShapeDtypeStruct((8, 128), jnp.int32)
        zero = call(ready_kernel, zeros, [own_one, beside_one, bias_one[:, None]], name="ready")
        total, zero = call(
            first_own_kernel,
            [partial, zeros],
            [kept, from_other_core(kept, core + zero[0, 0]), own_one],
            joined,
            cost_estimate=work,
            name="first_own",
        )
        later_core = core + zero[0, 0]
        total = call(
            first_near_kernel,
            partial,
            [near_plane, from_other_core(near_plane, later_core), beside_one, total],
            joined,
            cost_estimate=work,
            name="first_near",
        )
        hidden = call(
            first_far_kernel,
            jax.ShapeDtypeStruct((rows + RIM, full, lanes), BF16),
            [far_plane, from_other_core(far_plane, later_core), beside_one, total, bias_one[:, None]],
            joined,
            cost_estimate=work,
            name="first_far",
        )

        partial = jax.ShapeDtypeStruct((rows, CORES, groups * width, lanes), F32)
        work = cost(rows, 1, full, lanes)
        far_plane, near_plane = halo(hidden)
        total = call(second_own_kernel, partial, [hidden, own_two], cost_estimate=work, name="second_own")
        total = call(
            second_near_kernel, partial, [near_plane, beside_two, total], cost_estimate=work, name="second_near"
        )
        block = (rows, width, lanes)
        ends = [
            call(
                functools.partial(second_far_kernel, other),
                [jax.ShapeDtypeStruct(shape, BF16) for shape in shapes],
                [far_plane, beside_two, total, offsets_two],
                [pltpu.VMEM((groups, *block), BF16)],
                cost_estimate=cost(rows // 2, 1, full, lanes),
                name=name,
            )
            for other, shapes, name in (
                (True, [(groups, *block)], "second_far_other"),
                (False, [block] * groups, "second_far_own"),
            )
        ]
        swapped = lax.ppermute(ends[0][0], "chan", swap)
        blocks = [jnp.stack([ends[1][k], swapped[k]]) for k in range(groups)]
        blocks = [blocks[0]] + [lax.ppermute(blocks[k], "chan", ahead(k)) for k in range(1, groups)]
        return call(
            unpack_kernel,
            jax.ShapeDtypeStruct(volume.shape, BF16),
            blocks,
            [pltpu.VMEM((chan, rows, width, lanes), BF16)],
            name="unpack_rows",
        )

    placed = (P("chan", "space", None, None), P(), P(), P(), P())
    return jax.shard_map(
        per_device,
        mesh=mesh,
        in_specs=placed,
        out_specs=P("chan", "space", None, None),
        check_vma=False,
    )
```

```python
import functools

import jax
import jax.numpy as jnp
from jax import lax
from jax.experimental import pallas as pl
from jax.experimental.pallas import tpu as pltpu
from jax.sharding import PartitionSpec as P

BF16 = jnp.bfloat16
F32 = jnp.float32
CORES = 2
RIM = 2
FIRST = True
SECOND = True
PARAMS = pltpu.CompilerParams(vmem_limit_bytes=24 * 1024 * 1024)
VMEM = pl.BlockSpec(memory_space=pltpu.VMEM)


def my_group():
    return lax.axis_index("chan") // CORES


def my_core():
    return lax.axis_index("chan") % CORES


def along_lanes(total, lanes):
    chans = total.shape[0] // 3
    lane = lax.broadcasted_iota(jnp.int32, (chans, lanes), 1)
    low = pltpu.roll(total[:chans], 1, 1)
    high = pltpu.roll(total[2 * chans :], lanes - 1, 1)
    return (
        total[chans : 2 * chans]
        + jnp.where(lane == 0, 0.0, low)
        + jnp.where(lane == lanes - 1, 0.0, high)
    )


def conv_rows(get, planes, weight, store, rows, lanes):
    for start in range(0, rows, 2):
        parts = []
        for a in range(planes):
            for e in range(3):
                pair = [get(a, start + e + n) for n in range(2)]
                parts.append(jnp.concatenate(pair, axis=1))
        stacked = jnp.concatenate(parts, axis=0)
        total = jnp.dot(weight, stacked, preferred_element_type=F32)
        for n in range(2):
            store(start + n, along_lanes(total[:, n * lanes : (n + 1) * lanes], lanes))


def pack_kernel(volume_ref, *refs):
    outs, rows_ref = refs[:-1], refs[-1]
    width, _, length, lanes = volume_ref.shape
    groups = len(outs)
    rows = length // groups
    edge = jnp.zeros((RIM, width, lanes), BF16)
    rows_ref[:RIM] = edge
    rows_ref[RIM + length :] = edge
    turned = jnp.swapaxes(volume_ref[:, 0].astype(F32), 0, 1)
    rows_ref[RIM : RIM + length] = turned.astype(BF16)
    for k in range(groups):
        target = lax.rem(my_group() + k, groups)
        outs[k][0] = rows_ref[pl.ds(target * rows, rows + 2 * RIM)]


def gather_rows(kept_ref, other_ref, joined_ref):
    core = my_core()
    groups, rows, width, lanes = other_ref.shape
    offset = core * (kept_ref.shape[1] - rows)
    for row in range(rows):
        parts = []
        for g in range(groups):
            kept = kept_ref[g, offset + row]
            other = other_ref[g, row]
            parts += [jnp.where(core == 0, kept, other), jnp.where(core == 0, other, kept)]
        joined_ref[row] = jnp.concatenate(parts, axis=0)


def rows_of(ref, masked):
    def get(_, row):
        value = ref[row]
        if masked:
            plane = lax.axis_index("space")
            edge = (plane == 0) | (plane == lax.axis_size("space") - 1)
            value = jnp.where(edge, jnp.zeros_like(value), value)
        return value

    return get


def side_of(far):
    odd = lax.axis_index("space") % 2
    return odd if far else 1 - odd


def own_kernel(plane_ref, weight_ref, out_ref):
    rows, _, lanes = out_ref.shape

    def store(row, value):
        out_ref[row] = value

    conv_rows(rows_of(plane_ref, False), 1, weight_ref[...], store, rows, lanes)


def add_kernel(far, plane_ref, weight_ref, before_ref, out_ref):
    rows, _, lanes = out_ref.shape

    def store(row, value):
        out_ref[row] = before_ref[row] + value

    conv_rows(rows_of(plane_ref, far), 1, weight_ref[side_of(far)], store, rows, lanes)


def first_own_kernel(kept_ref, other_ref, weight_ref, later_ref, bias_ref, out_ref, zero_ref, joined_ref):
    gather_rows(kept_ref, other_ref, joined_ref)
    own_kernel(joined_ref, weight_ref, out_ref)
    zero_ref[...] = jnp.zeros_like(zero_ref)


def first_add_kernel(far, kept_ref, other_ref, weight_ref, before_ref, out_ref, joined_ref):
    gather_rows(kept_ref, other_ref, joined_ref)
    add_kernel(far, joined_ref, weight_ref, before_ref, out_ref)


def first_kernel(far, kept_ref, other_ref, weight_ref, before_ref, bias_ref, out_ref, joined_ref):
    gather_rows(kept_ref, other_ref, joined_ref)
    rows, _, lanes = out_ref.shape
    block = lax.axis_index("chan")
    bias = bias_ref[...]

    def store(row, value):
        value = jnp.maximum(value + before_ref[row] + bias, 0.0)
        if row == 0:
            value = jnp.where(block == 0, 0.0, value)
        if row == rows - 1:
            value = jnp.where(block == lax.axis_size("chan") - 1, 0.0, value)
        out_ref[row] = value.astype(BF16)

    conv_rows(rows_of(joined_ref, far), 1, weight_ref[side_of(far)], store, rows, lanes)


def second_kernel(far, plane_ref, weight_ref, before_ref, bias_ref, *refs):
    outs, all_ref = refs[:-1], refs[-1]
    groups, cores, rows, width, lanes = all_ref.shape
    bias = bias_ref[...]

    def store(row, value):
        value = jnp.maximum(value + before_ref[row] + bias, 0.0).astype(BF16)
        for g in range(groups):
            for c in range(cores):
                at = (g * cores + c) * width
                all_ref[g, c, row] = value[at : at + width]

    conv_rows(rows_of(plane_ref, far), 1, weight_ref[side_of(far)], store, rows, lanes)
    for k in range(groups):
        outs[k][...] = all_ref[lax.rem(my_group() + k, groups)]


def unpack_kernel(swapped_ref, *refs):
    blocks, out_ref, rows_ref = refs[:-2], refs[-2], refs[-1]
    groups = len(blocks)
    _, rows, width, lanes = blocks[0].shape
    group, core = my_group(), my_core()
    for k in range(groups):
        source = lax.rem(group + groups - k, groups) * CORES
        rows_ref[source + core] = blocks[k][core]
        rows_ref[source + 1 - core] = swapped_ref[k]
    length = groups * CORES * rows
    turned = rows_ref[...].reshape(length, width, lanes).astype(F32)
    out_ref[:, 0] = jnp.swapaxes(turned, 0, 1).astype(BF16)


def arranged(weight):
    _, inner, outer = weight.shape
    taps = weight.reshape(3, 3, 3, inner, outer)
    own = taps[1].transpose(1, 3, 0, 2).reshape(3 * outer, 3 * inner)
    beside = taps[::2].transpose(0, 2, 4, 1, 3).reshape(2, 3 * outer, 3 * inner)
    return own, beside


def cost(rows, planes, full, lanes):
    flops = 2 * rows * lanes * full * full * 9 * planes
    return pl.CostEstimate(flops=flops, bytes_accessed=4_000_000, transcendentals=0)


def solution(mesh):
    space = mesh.shape["space"]
    chan = mesh.shape["chan"]
    groups = chan // CORES
    swap = [(i, i ^ 1) for i in range(chan)]

    near = [(i, i ^ 1) for i in range(space)]

    def far_partner(i, j):
        if i in (0, space - 1):
            return i * chan + (j ^ 1)
        return (((i - 1) ^ 1) + 1) * chan + j

    far = [(i * chan + j, far_partner(i, j)) for i in range(space) for j in range(chan)]

    def ahead(k):
        return [(i, (i + CORES * k) % chan) for i in range(chan)]

    def call(kernel, shapes, inputs, scratch=(), **kwargs):
        single = not isinstance(shapes, list)
        return pl.pallas_call(
            kernel,
            out_shape=shapes,
            in_specs=[VMEM] * len(inputs),
            out_specs=VMEM if single else [VMEM] * len(shapes),
            scratch_shapes=scratch,
            compiler_params=PARAMS,
            **kwargs,
        )(*inputs)

    def per_device(volume, weight_one, bias_one, weight_two, bias_two):
        width, _, length, lanes = volume.shape
        full = width * chan
        rows = length // chan
        index = lax.axis_index("chan")
        group, core = index // CORES, index % CORES

        own_one, beside_one = arranged(weight_one)
        own_two, beside_two = arranged(weight_two)

        tall = CORES * rows + 2 * RIM
        pieces = call(
            pack_kernel,
            [jax.ShapeDtypeStruct((1, tall, width, lanes), BF16)] * groups,
            [volume],
            [pltpu.VMEM((length + 2 * RIM, width, lanes), BF16)],
            name="pack_rows",
        )
        kept = jnp.zeros((groups, tall, width, lanes), BF16)
        kept = lax.dynamic_update_slice_in_dim(kept, pieces[0], group, 0)
        for k in range(1, groups):
            got = lax.ppermute(pieces[k], "chan", ahead(k))
            kept = lax.dynamic_update_slice_in_dim(kept, got, (group + groups - k) % groups, 0)

        def from_other_core(array, core):
            sent = lax.dynamic_slice_in_dim(array, (1 - core) * rows, rows + 2 * RIM, 1)
            return lax.ppermute(sent, "chan", swap)

        def halo(array, far_first):
            far_plane = lax.ppermute(array, ("space", "chan"), far)
            near_plane = lax.ppermute(array, "space", near)
            return (far_plane, near_plane) if far_first else (near_plane, far_plane)

        partial = jax.ShapeDtypeStruct((rows + RIM, full, lanes), F32)
        joined = [pltpu.VMEM((rows + 2 * RIM, full, lanes), BF16)]
        work = cost(rows + RIM, 1, full, lanes)
        planes = halo(kept, FIRST)
        total, zero = call(
            first_own_kernel,
            [partial, jax.ShapeDtypeStruct((8, 128), jnp.int32)],
            [kept, from_other_core(kept, core), own_one, beside_one, bias_one[:, None]],
            joined,
            cost_estimate=work,
            name="first_own",
        )
        later_core = core + zero[0, 0]
        total = call(
            functools.partial(first_add_kernel, FIRST),
            partial,
            [planes[0], from_other_core(planes[0], later_core), beside_one, total],
            joined,
            cost_estimate=work,
            name="first_add",
        )
        hidden = call(
            functools.partial(first_kernel, not FIRST),
            jax.ShapeDtypeStruct((rows + RIM, full, lanes), BF16),
            [planes[1], from_other_core(planes[1], later_core), beside_one, total, bias_one[:, None]],
            joined,
            cost_estimate=work,
            name="first_last",
        )

        partial = jax.ShapeDtypeStruct((rows, full, lanes), F32)
        work = cost(rows, 1, full, lanes)
        planes = halo(hidden, SECOND)
        total = call(own_kernel, partial, [hidden, own_two], cost_estimate=work, name="second_own")
        total = call(
            functools.partial(add_kernel, SECOND), partial, [planes[0], beside_two, total], cost_estimate=work, name="second_add"
        )
        blocks = call(
            functools.partial(second_kernel, not SECOND),
            [jax.ShapeDtypeStruct((CORES, rows, width, lanes), BF16)] * groups,
            [planes[1], beside_two, total, bias_two[:, None]],
            [pltpu.VMEM((groups, CORES, rows, width, lanes), BF16)],
            cost_estimate=work,
            name="second_last",
        )

        blocks = [blocks[0]] + [lax.ppermute(blocks[k], "chan", ahead(k)) for k in range(1, groups)]
        theirs = jnp.stack([lax.dynamic_index_in_dim(b, 1 - core, 0, keepdims=False) for b in blocks])
        swapped = lax.ppermute(theirs, "chan", swap)
        return call(
            unpack_kernel,
            jax.ShapeDtypeStruct(volume.shape, BF16),
            [swapped, *blocks],
            [pltpu.VMEM((chan, rows, width, lanes), BF16)],
            name="unpack_rows",
        )

    placed = (P("chan", "space", None, None), P(), P(), P(), P())
    return jax.shard_map(
        per_device,
        mesh=mesh,
        in_specs=placed,
        out_specs=P("chan", "space", None, None),
        check_vma=False,
    )
```

```python
import functools

import jax
import jax.numpy as jnp
from jax import lax
from jax.experimental import pallas as pl
from jax.experimental.pallas import tpu as pltpu
from jax.sharding import PartitionSpec as P

BF16 = jnp.bfloat16
F32 = jnp.float32
CORES = 2
RIM = 2
PARAMS = pltpu.CompilerParams(vmem_limit_bytes=24 * 1024 * 1024)
VMEM = pl.BlockSpec(memory_space=pltpu.VMEM)


def my_group():
    return lax.axis_index("chan") // CORES


def my_core():
    return lax.axis_index("chan") % CORES


def along_lanes(total, lanes):
    chans = total.shape[0] // 3
    lane = lax.broadcasted_iota(jnp.int32, (chans, lanes), 1)
    low = pltpu.roll(total[:chans], 1, 1)
    high = pltpu.roll(total[2 * chans :], lanes - 1, 1)
    return (
        total[chans : 2 * chans]
        + jnp.where(lane == 0, 0.0, low)
        + jnp.where(lane == lanes - 1, 0.0, high)
    )


def conv_rows(get, planes, weight, store, rows, lanes):
    for start in range(0, rows, 2):
        parts = []
        for a in range(planes):
            for e in range(3):
                pair = [get(a, start + e + n) for n in range(2)]
                parts.append(jnp.concatenate(pair, axis=1))
        stacked = jnp.concatenate(parts, axis=0)
        total = jnp.dot(weight, stacked, preferred_element_type=F32)
        for n in range(2):
            store(start + n, along_lanes(total[:, n * lanes : (n + 1) * lanes], lanes))


def pack_kernel(volume_ref, *refs):
    outs, rows_ref = refs[:-1], refs[-1]
    width, _, length, lanes = volume_ref.shape
    groups = len(outs)
    rows = length // groups
    edge = jnp.zeros((RIM, width, lanes), BF16)
    rows_ref[:RIM] = edge
    rows_ref[RIM + length :] = edge
    turned = jnp.swapaxes(volume_ref[:, 0].astype(F32), 0, 1)
    rows_ref[RIM : RIM + length] = turned.astype(BF16)
    for k in range(groups):
        target = lax.rem(my_group() + k, groups)
        outs[k][0] = rows_ref[pl.ds(target * rows, rows + 2 * RIM)]


def gather_rows(kept_ref, other_ref, joined_ref):
    core = my_core()
    groups, rows, width, lanes = other_ref.shape
    offset = core * (kept_ref.shape[1] - rows)
    for row in range(rows):
        parts = []
        for g in range(groups):
            kept = kept_ref[g, offset + row]
            other = other_ref[g, row]
            parts += [jnp.where(core == 0, kept, other), jnp.where(core == 0, other, kept)]
        joined_ref[row] = jnp.concatenate(parts, axis=0)


def rows_of(ref, masked):
    def get(_, row):
        value = ref[row]
        if masked:
            plane = lax.axis_index("space")
            edge = (plane == 0) | (plane == lax.axis_size("space") - 1)
            value = jnp.where(edge, jnp.zeros_like(value), value)
        return value

    return get


def own_kernel(plane_ref, weight_ref, out_ref):
    rows, _, lanes = out_ref.shape

    def store(row, value):
        out_ref[row] = value

    conv_rows(rows_of(plane_ref, False), 1, weight_ref[...], store, rows, lanes)


def near_kernel(plane_ref, weight_ref, before_ref, out_ref):
    rows, _, lanes = out_ref.shape

    def store(row, value):
        out_ref[row] = before_ref[row] + value

    weight = weight_ref[1 - lax.axis_index("space") % 2]
    conv_rows(rows_of(plane_ref, False), 1, weight, store, rows, lanes)


def first_own_kernel(kept_ref, other_ref, weight_ref, *refs):
    out_ref, zero_ref, joined_ref = refs[-3:]
    gather_rows(kept_ref, other_ref, joined_ref)
    own_kernel(joined_ref, weight_ref, out_ref)
    zero_ref[...] = jnp.zeros_like(zero_ref)


def first_near_kernel(kept_ref, other_ref, weight_ref, before_ref, out_ref, joined_ref):
    gather_rows(kept_ref, other_ref, joined_ref)
    near_kernel(joined_ref, weight_ref, before_ref, out_ref)


def first_far_kernel(kept_ref, other_ref, weight_ref, before_ref, bias_ref, out_ref, joined_ref):
    gather_rows(kept_ref, other_ref, joined_ref)
    rows, _, lanes = out_ref.shape
    block = lax.axis_index("chan")
    bias = bias_ref[...]

    def store(row, value):
        value = jnp.maximum(value + before_ref[row] + bias, 0.0)
        if row == 0:
            value = jnp.where(block == 0, 0.0, value)
        if row == rows - 1:
            value = jnp.where(block == lax.axis_size("chan") - 1, 0.0, value)
        out_ref[row] = value.astype(BF16)

    weight = weight_ref[lax.axis_index("space") % 2]
    conv_rows(rows_of(joined_ref, True), 1, weight, store, rows, lanes)


def share_kernel(far, plane_ref, weight_ref, *refs):
    out_ref = refs[-1]
    rows, _, lanes = out_ref.shape
    odd = lax.axis_index("space") % 2

    def store(row, value):
        out_ref[row] = value.astype(BF16)

    weight = weight_ref[1 - odd if far else odd]
    conv_rows(rows_of(plane_ref, False), 1, weight, store, rows, lanes)


def sum_kernel(far_ref, own_ref, out_ref):
    far = rows_of(far_ref, True)
    for row in range(out_ref.shape[0]):
        out_ref[row] = own_ref[row] + far(0, row).astype(F32)


def second_kernel(near_ref, own_ref, bias_ref, *refs):
    outs, all_ref = refs[:-1], refs[-1]
    groups, cores, rows, width, _ = all_ref.shape
    bias = bias_ref[...]
    for row in range(rows):
        value = own_ref[row] + near_ref[row].astype(F32)
        value = jnp.maximum(value + bias, 0.0).astype(BF16)
        for g in range(groups):
            for c in range(cores):
                at = (g * cores + c) * width
                all_ref[g, c, row] = value[at : at + width]
    for k in range(groups):
        outs[k][...] = all_ref[lax.rem(my_group() + k, groups)]


def unpack_kernel(swapped_ref, *refs):
    blocks, out_ref, rows_ref = refs[:-2], refs[-2], refs[-1]
    groups = len(blocks)
    _, rows, width, lanes = blocks[0].shape
    group, core = my_group(), my_core()
    for k in range(groups):
        source = lax.rem(group + groups - k, groups) * CORES
        rows_ref[source + core] = blocks[k][core]
        rows_ref[source + 1 - core] = swapped_ref[k]
    length = groups * CORES * rows
    turned = rows_ref[...].reshape(length, width, lanes).astype(F32)
    out_ref[:, 0] = jnp.swapaxes(turned, 0, 1).astype(BF16)


def arranged(weight):
    _, inner, outer = weight.shape
    taps = weight.reshape(3, 3, 3, inner, outer)
    own = taps[1].transpose(1, 3, 0, 2).reshape(3 * outer, 3 * inner)
    beside = taps[::2].transpose(0, 2, 4, 1, 3).reshape(2, 3 * outer, 3 * inner)
    return own, beside


def cost(rows, planes, full, lanes):
    flops = 2 * rows * lanes * full * full * 9 * planes
    return pl.CostEstimate(flops=flops, bytes_accessed=4_000_000, transcendentals=0)


def solution(mesh):
    space = mesh.shape["space"]
    chan = mesh.shape["chan"]
    groups = chan // CORES
    swap = [(i, i ^ 1) for i in range(chan)]

    near = [(i, i ^ 1) for i in range(space)]

    def far_partner(i, j):
        if i in (0, space - 1):
            return i * chan + (j ^ 1)
        return (((i - 1) ^ 1) + 1) * chan + j

    far = [(i * chan + j, far_partner(i, j)) for i in range(space) for j in range(chan)]

    def ahead(k):
        return [(i, (i + CORES * k) % chan) for i in range(chan)]

    def call(kernel, shapes, inputs, scratch=(), **kwargs):
        single = not isinstance(shapes, list)
        return pl.pallas_call(
            kernel,
            out_shape=shapes,
            in_specs=[VMEM] * len(inputs),
            out_specs=VMEM if single else [VMEM] * len(shapes),
            scratch_shapes=scratch,
            compiler_params=PARAMS,
            **kwargs,
        )(*inputs)

    def per_device(volume, weight_one, bias_one, weight_two, bias_two):
        width, _, length, lanes = volume.shape
        full = width * chan
        rows = length // chan
        index = lax.axis_index("chan")
        group, core = index // CORES, index % CORES

        own_one, beside_one = arranged(weight_one)
        own_two, beside_two = arranged(weight_two)

        tall = CORES * rows + 2 * RIM
        pieces = call(
            pack_kernel,
            [jax.ShapeDtypeStruct((1, tall, width, lanes), BF16)] * groups,
            [volume],
            [pltpu.VMEM((length + 2 * RIM, width, lanes), BF16)],
            name="pack_rows",
        )
        kept = jnp.zeros((groups, tall, width, lanes), BF16)
        kept = lax.dynamic_update_slice_in_dim(kept, pieces[0], group, 0)
        for k in range(1, groups):
            got = lax.ppermute(pieces[k], "chan", ahead(k))
            kept = lax.dynamic_update_slice_in_dim(kept, got, (group + groups - k) % groups, 0)

        def from_other_core(array, core):
            sent = lax.dynamic_slice_in_dim(array, (1 - core) * rows, rows + 2 * RIM, 1)
            return lax.ppermute(sent, "chan", swap)

        partial = jax.ShapeDtypeStruct((rows + RIM, full, lanes), F32)
        joined = [pltpu.VMEM((rows + 2 * RIM, full, lanes), BF16)]
        work = cost(rows + RIM, 1, full, lanes)
        far_plane = lax.ppermute(kept, ("space", "chan"), far)
        near_plane = lax.ppermute(kept, "space", near)
        total, zero = call(
            first_own_kernel,
            [partial, jax.ShapeDtypeStruct((8, 128), jnp.int32)],
            [kept, from_other_core(kept, core), own_one, beside_one, bias_one[:, None], beside_two],
            joined,
            cost_estimate=work,
            name="first_own",
        )
        later_core = core + zero[0, 0]
        total = call(
            first_near_kernel,
            partial,
            [near_plane, from_other_core(near_plane, later_core), beside_one, total],
            joined,
            cost_estimate=work,
            name="first_near",
        )
        hidden = call(
            first_far_kernel,
            jax.ShapeDtypeStruct((rows + RIM, full, lanes), BF16),
            [far_plane, from_other_core(far_plane, later_core), beside_one, total, bias_one[:, None]],
            joined,
            cost_estimate=work,
            name="first_far",
        )

        work = cost(rows, 1, full, lanes)
        sent = jax.ShapeDtypeStruct((rows, full, lanes), BF16)
        far_share = call(
            functools.partial(share_kernel, True), sent, [hidden, beside_two], cost_estimate=work, name="far_share"
        )
        near_share = call(
            functools.partial(share_kernel, False),
            sent,
            [hidden, beside_two, far_share],
            cost_estimate=work,
            name="near_share",
        )
        far_share = lax.ppermute(far_share, ("space", "chan"), far)
        near_share = lax.ppermute(near_share, "space", near)
        partial = jax.ShapeDtypeStruct((rows, full, lanes), F32)
        total = call(own_kernel, partial, [hidden, own_two], cost_estimate=work, name="second_own")
        total = call(sum_kernel, partial, [far_share, total], name="second_far")
        blocks = call(
            second_kernel,
            [jax.ShapeDtypeStruct((CORES, rows, width, lanes), BF16)] * groups,
            [near_share, total, bias_two[:, None]],
            [pltpu.VMEM((groups, CORES, rows, width, lanes), BF16)],
            name="second_sum",
        )

        blocks = [blocks[0]] + [lax.ppermute(blocks[k], "chan", ahead(k)) for k in range(1, groups)]
        theirs = jnp.stack([lax.dynamic_index_in_dim(b, 1 - core, 0, keepdims=False) for b in blocks])
        swapped = lax.ppermute(theirs, "chan", swap)
        return call(
            unpack_kernel,
            jax.ShapeDtypeStruct(volume.shape, BF16),
            [swapped, *blocks],
            [pltpu.VMEM((chan, rows, width, lanes), BF16)],
            name="unpack_rows",
        )

    placed = (P("chan", "space", None, None), P(), P(), P(), P())
    return jax.shard_map(
        per_device,
        mesh=mesh,
        in_specs=placed,
        out_specs=P("chan", "space", None, None),
        check_vma=False,
    )
```

```python
import jax
import jax.numpy as jnp
from jax import lax
from jax.experimental import pallas as pl
from jax.experimental.pallas import tpu as pltpu
from jax.sharding import PartitionSpec as P

BF16 = jnp.bfloat16
F32 = jnp.float32
CORES = 2
RIM = 2
PARAMS = pltpu.CompilerParams(vmem_limit_bytes=24 * 1024 * 1024)
VMEM = pl.BlockSpec(memory_space=pltpu.VMEM)


def my_group():
    return lax.axis_index("chan") // CORES


def my_core():
    return lax.axis_index("chan") % CORES


def along_lanes(total, lanes):
    chans = total.shape[0] // 3
    lane = lax.broadcasted_iota(jnp.int32, (chans, lanes), 1)
    low = pltpu.roll(total[:chans], 1, 1)
    high = pltpu.roll(total[2 * chans :], lanes - 1, 1)
    return (
        total[chans : 2 * chans]
        + jnp.where(lane == 0, 0.0, low)
        + jnp.where(lane == lanes - 1, 0.0, high)
    )


def conv_rows(get, planes, weight, store, rows, lanes):
    for start in range(0, rows, 2):
        parts = []
        for a in range(planes):
            for e in range(3):
                pair = [get(a, start + e + n) for n in range(2)]
                parts.append(jnp.concatenate(pair, axis=1))
        stacked = jnp.concatenate(parts, axis=0)
        total = jnp.dot(weight, stacked, preferred_element_type=F32)
        for n in range(2):
            store(start + n, along_lanes(total[:, n * lanes : (n + 1) * lanes], lanes))


def pack_kernel(volume_ref, *refs):
    outs, rows_ref = refs[:-1], refs[-1]
    width, _, length, lanes = volume_ref.shape
    groups = len(outs)
    rows = length // groups
    edge = jnp.zeros((RIM, width, lanes), BF16)
    rows_ref[:RIM] = edge
    rows_ref[RIM + length :] = edge
    turned = jnp.swapaxes(volume_ref[:, 0].astype(F32), 0, 1)
    rows_ref[RIM : RIM + length] = turned.astype(BF16)
    for k in range(groups):
        target = lax.rem(my_group() + k, groups)
        outs[k][0] = rows_ref[pl.ds(target * rows, rows + 2 * RIM)]


def gather_rows(kept_ref, other_ref, joined_ref):
    core = my_core()
    groups, rows, width, lanes = other_ref.shape
    offset = core * (kept_ref.shape[1] - rows)
    for row in range(rows):
        parts = []
        for g in range(groups):
            kept = kept_ref[g, offset + row]
            other = other_ref[g, row]
            parts += [jnp.where(core == 0, kept, other), jnp.where(core == 0, other, kept)]
        joined_ref[row] = jnp.concatenate(parts, axis=0)


def rows_of(ref, masked):
    def get(_, row):
        value = ref[row]
        if masked:
            plane = lax.axis_index("space")
            edge = (plane == 0) | (plane == lax.axis_size("space") - 1)
            value = jnp.where(edge, jnp.zeros_like(value), value)
        return value

    return get


def own_kernel(plane_ref, weight_ref, out_ref):
    rows, _, lanes = out_ref.shape

    def store(row, value):
        out_ref[row] = value

    conv_rows(rows_of(plane_ref, False), 1, weight_ref[...], store, rows, lanes)


def near_kernel(plane_ref, weight_ref, before_ref, out_ref):
    rows, _, lanes = out_ref.shape

    def store(row, value):
        out_ref[row] = before_ref[row] + value

    weight = weight_ref[1 - lax.axis_index("space") % 2]
    conv_rows(rows_of(plane_ref, False), 1, weight, store, rows, lanes)


def first_own_kernel(kept_ref, other_ref, weight_ref, later_ref, bias_ref, out_ref, zero_ref, joined_ref):
    gather_rows(kept_ref, other_ref, joined_ref)
    own_kernel(joined_ref, weight_ref, out_ref)
    zero_ref[...] = jnp.zeros_like(zero_ref)


def first_near_kernel(kept_ref, other_ref, weight_ref, before_ref, out_ref, joined_ref):
    gather_rows(kept_ref, other_ref, joined_ref)
    near_kernel(joined_ref, weight_ref, before_ref, out_ref)


def first_far_kernel(kept_ref, other_ref, weight_ref, before_ref, bias_ref, out_ref, joined_ref):
    gather_rows(kept_ref, other_ref, joined_ref)
    rows, _, lanes = out_ref.shape
    block = lax.axis_index("chan")
    bias = bias_ref[...]

    def store(row, value):
        value = jnp.maximum(value + before_ref[row] + bias, 0.0)
        if row == 0:
            value = jnp.where(block == 0, 0.0, value)
        if row == rows - 1:
            value = jnp.where(block == lax.axis_size("chan") - 1, 0.0, value)
        out_ref[row] = value.astype(BF16)

    weight = weight_ref[lax.axis_index("space") % 2]
    conv_rows(rows_of(joined_ref, True), 1, weight, store, rows, lanes)


def second_kernel(plane_ref, weight_ref, before_ref, bias_ref, *refs):
    outs, all_ref = refs[:-1], refs[-1]
    groups, cores, rows, width, lanes = all_ref.shape
    bias = bias_ref[...]

    def store(row, value):
        value = jnp.maximum(value + before_ref[row] + bias, 0.0).astype(BF16)
        for g in range(groups):
            for c in range(cores):
                at = (g * cores + c) * width
                all_ref[g, c, row] = value[at : at + width]

    weight = weight_ref[lax.axis_index("space") % 2]
    conv_rows(rows_of(plane_ref, True), 1, weight, store, rows, lanes)
    for k in range(groups):
        outs[k][...] = all_ref[lax.rem(my_group() + k, groups)]


def unpack_kernel(swapped_ref, *refs):
    blocks, out_ref, rows_ref = refs[:-2], refs[-2], refs[-1]
    groups = len(blocks)
    _, rows, width, lanes = blocks[0].shape
    group, core = my_group(), my_core()
    for k in range(groups):
        source = lax.rem(group + groups - k, groups) * CORES
        rows_ref[source + core] = blocks[k][core]
        rows_ref[source + 1 - core] = swapped_ref[k]
    length = groups * CORES * rows
    turned = rows_ref[...].reshape(length, width, lanes).astype(F32)
    out_ref[:, 0] = jnp.swapaxes(turned, 0, 1).astype(BF16)


def arranged(weight):
    _, inner, outer = weight.shape
    taps = weight.reshape(3, 3, 3, inner, outer)
    own = taps[1].transpose(1, 3, 0, 2).reshape(3 * outer, 3 * inner)
    beside = taps[::2].transpose(0, 2, 4, 1, 3).reshape(2, 3 * outer, 3 * inner)
    return own, beside


def cost(rows, planes, full, lanes):
    flops = 2 * rows * lanes * full * full * 9 * planes
    return pl.CostEstimate(flops=flops, bytes_accessed=4_000_000, transcendentals=0)


def solution(mesh):
    space = mesh.shape["space"]
    chan = mesh.shape["chan"]
    groups = chan // CORES
    swap = [(i, i ^ 1) for i in range(chan)]

    near = [(i, i ^ 1) for i in range(space)]

    def far_partner(i, j):
        if i in (0, space - 1):
            return i * chan + (j ^ 1)
        return (((i - 1) ^ 1) + 1) * chan + j

    far = [(i * chan + j, far_partner(i, j)) for i in range(space) for j in range(chan)]

    def ahead(k):
        return [(i, (i + CORES * k) % chan) for i in range(chan)]

    def call(kernel, shapes, inputs, scratch=(), **kwargs):
        single = not isinstance(shapes, list)
        return pl.pallas_call(
            kernel,
            out_shape=shapes,
            in_specs=[VMEM] * len(inputs),
            out_specs=VMEM if single else [VMEM] * len(shapes),
            scratch_shapes=scratch,
            compiler_params=PARAMS,
            **kwargs,
        )(*inputs)

    def per_device(volume, weight_one, bias_one, weight_two, bias_two):
        width, _, length, lanes = volume.shape
        full = width * chan
        rows = length // chan
        index = lax.axis_index("chan")
        group, core = index // CORES, index % CORES

        own_one, beside_one = arranged(weight_one)
        own_two, beside_two = arranged(weight_two)

        tall = CORES * rows + 2 * RIM
        pieces = call(
            pack_kernel,
            [jax.ShapeDtypeStruct((1, tall, width, lanes), BF16)] * groups,
            [volume],
            [pltpu.VMEM((length + 2 * RIM, width, lanes), BF16)],
            name="pack_rows",
        )
        kept = jnp.zeros((groups, tall, width, lanes), BF16)
        kept = lax.dynamic_update_slice_in_dim(kept, pieces[0], group, 0)
        for k in sorted(range(1, groups), key=lambda k: abs(k - groups // 2)):
            got = lax.ppermute(pieces[k], "chan", ahead(k))
            kept = lax.dynamic_update_slice_in_dim(kept, got, (group + groups - k) % groups, 0)

        def from_other_core(array, core):
            sent = lax.dynamic_slice_in_dim(array, (1 - core) * rows, rows + 2 * RIM, 1)
            return lax.ppermute(sent, "chan", swap)

        def halo(array):
            return lax.ppermute(array, ("space", "chan"), far), lax.ppermute(array, "space", near)

        partial = jax.ShapeDtypeStruct((rows + RIM, full, lanes), F32)
        joined = [pltpu.VMEM((rows + 2 * RIM, full, lanes), BF16)]
        work = cost(rows + RIM, 1, full, lanes)
        far_plane, near_plane = halo(kept)
        total, zero = call(
            first_own_kernel,
            [partial, jax.ShapeDtypeStruct((8, 128), jnp.int32)],
            [kept, from_other_core(kept, core), own_one, beside_one, bias_one[:, None]],
            joined,
            cost_estimate=work,
            name="first_own",
        )
        later_core = core + zero[0, 0]
        total = call(
            first_near_kernel,
            partial,
            [near_plane, from_other_core(near_plane, later_core), beside_one, total],
            joined,
            cost_estimate=work,
            name="first_near",
        )
        hidden = call(
            first_far_kernel,
            jax.ShapeDtypeStruct((rows + RIM, full, lanes), BF16),
            [far_plane, from_other_core(far_plane, later_core), beside_one, total, bias_one[:, None]],
            joined,
            cost_estimate=work,
            name="first_far",
        )

        partial = jax.ShapeDtypeStruct((rows, full, lanes), F32)
        work = cost(rows, 1, full, lanes)
        far_plane, near_plane = halo(hidden)
        total = call(own_kernel, partial, [hidden, own_two], cost_estimate=work, name="second_own")
        total = call(near_kernel, partial, [near_plane, beside_two, total], cost_estimate=work, name="second_near")
        blocks = call(
            second_kernel,
            [jax.ShapeDtypeStruct((CORES, rows, width, lanes), BF16)] * groups,
            [far_plane, beside_two, total, bias_two[:, None]],
            [pltpu.VMEM((groups, CORES, rows, width, lanes), BF16)],
            cost_estimate=work,
            name="second_far",
        )

        blocks = [blocks[0]] + [lax.ppermute(blocks[k], "chan", ahead(k)) for k in range(1, groups)]
        theirs = jnp.stack([lax.dynamic_index_in_dim(b, 1 - core, 0, keepdims=False) for b in blocks])
        swapped = lax.ppermute(theirs, "chan", swap)
        return call(
            unpack_kernel,
            jax.ShapeDtypeStruct(volume.shape, BF16),
            [swapped, *blocks],
            [pltpu.VMEM((chan, rows, width, lanes), BF16)],
            name="unpack_rows",
        )

    placed = (P("chan", "space", None, None), P(), P(), P(), P())
    return jax.shard_map(
        per_device,
        mesh=mesh,
        in_specs=placed,
        out_specs=P("chan", "space", None, None),
        check_vma=False,
    )
```

```python
import jax
import jax.numpy as jnp
from jax import lax
from jax.experimental import pallas as pl
from jax.experimental.pallas import tpu as pltpu
from jax.sharding import PartitionSpec as P

BF16 = jnp.bfloat16
F32 = jnp.float32
CORES = 2
RIM = 2
PARAMS = pltpu.CompilerParams(vmem_limit_bytes=24 * 1024 * 1024)
VMEM = pl.BlockSpec(memory_space=pltpu.VMEM)


def my_group():
    return lax.axis_index("chan") // CORES


def my_core():
    return lax.axis_index("chan") % CORES


def along_lanes(total, lanes):
    chans = total.shape[0] // 3
    lane = lax.broadcasted_iota(jnp.int32, (chans, lanes), 1)
    low = pltpu.roll(total[:chans], 1, 1)
    high = pltpu.roll(total[2 * chans :], lanes - 1, 1)
    return (
        total[chans : 2 * chans]
        + jnp.where(lane == 0, 0.0, low)
        + jnp.where(lane == lanes - 1, 0.0, high)
    )


def conv_rows(get, planes, weight, store, rows, lanes):
    for start in range(0, rows, 2):
        parts = []
        for a in range(planes):
            for e in range(3):
                pair = [get(a, start + e + n) for n in range(2)]
                parts.append(jnp.concatenate(pair, axis=1))
        stacked = jnp.concatenate(parts, axis=0)
        total = jnp.dot(weight, stacked, preferred_element_type=F32)
        for n in range(2):
            store(start + n, along_lanes(total[:, n * lanes : (n + 1) * lanes], lanes))


def pack_kernel(volume_ref, *refs):
    outs, rows_ref = refs[:-1], refs[-1]
    width, _, length, lanes = volume_ref.shape
    groups = len(outs)
    rows = length // groups
    edge = jnp.zeros((RIM, width, lanes), BF16)
    rows_ref[:RIM] = edge
    rows_ref[RIM + length :] = edge
    turned = jnp.swapaxes(volume_ref[:, 0].astype(F32), 0, 1)
    rows_ref[RIM : RIM + length] = turned.astype(BF16)
    for k in range(groups):
        target = lax.rem(my_group() + k, groups)
        outs[k][0] = rows_ref[pl.ds(target * rows, rows + 2 * RIM)]


def gather_rows(kept_ref, other_ref, joined_ref):
    core = my_core()
    groups, rows, width, lanes = other_ref.shape
    offset = core * (kept_ref.shape[1] - rows)
    for row in range(rows):
        parts = []
        for g in range(groups):
            kept = kept_ref[g, offset + row]
            other = other_ref[g, row]
            parts += [jnp.where(core == 0, kept, other), jnp.where(core == 0, other, kept)]
        joined_ref[row] = jnp.concatenate(parts, axis=0)


def rows_of(ref, masked):
    def get(_, row):
        value = ref[row]
        if masked:
            plane = lax.axis_index("space")
            edge = (plane == 0) | (plane == lax.axis_size("space") - 1)
            value = jnp.where(edge, jnp.zeros_like(value), value)
        return value

    return get


def own_kernel(plane_ref, weight_ref, out_ref):
    rows, _, lanes = out_ref.shape

    def store(row, value):
        out_ref[row] = value

    conv_rows(rows_of(plane_ref, False), 1, weight_ref[...], store, rows, lanes)


def near_kernel(plane_ref, weight_ref, before_ref, out_ref):
    rows, _, lanes = out_ref.shape

    def store(row, value):
        out_ref[row] = before_ref[row] + value

    weight = weight_ref[1 - lax.axis_index("space") % 2]
    conv_rows(rows_of(plane_ref, False), 1, weight, store, rows, lanes)


def first_own_kernel(kept_ref, other_ref, weight_ref, later_ref, bias_ref, out_ref, zero_ref, joined_ref):
    gather_rows(kept_ref, other_ref, joined_ref)
    own_kernel(joined_ref, weight_ref, out_ref)
    zero_ref[...] = jnp.zeros_like(zero_ref)


def first_near_kernel(kept_ref, other_ref, weight_ref, before_ref, out_ref, joined_ref):
    gather_rows(kept_ref, other_ref, joined_ref)
    near_kernel(joined_ref, weight_ref, before_ref, out_ref)


def first_far_kernel(kept_ref, other_ref, weight_ref, before_ref, bias_ref, out_ref, joined_ref):
    gather_rows(kept_ref, other_ref, joined_ref)
    rows, _, lanes = out_ref.shape
    block = lax.axis_index("chan")
    bias = bias_ref[...]

    def store(row, value):
        value = jnp.maximum(value + before_ref[row] + bias, 0.0)
        if row == 0:
            value = jnp.where(block == 0, 0.0, value)
        if row == rows - 1:
            value = jnp.where(block == lax.axis_size("chan") - 1, 0.0, value)
        out_ref[row] = value.astype(BF16)

    weight = weight_ref[lax.axis_index("space") % 2]
    conv_rows(rows_of(joined_ref, True), 1, weight, store, rows, lanes)


def second_kernel(plane_ref, weight_ref, before_ref, bias_ref, *refs):
    outs, all_ref = refs[:-1], refs[-1]
    groups, cores, rows, width, lanes = all_ref.shape
    bias = bias_ref[...]

    def store(row, value):
        value = jnp.maximum(value + before_ref[row] + bias, 0.0).astype(BF16)
        for g in range(groups):
            for c in range(cores):
                at = (g * cores + c) * width
                all_ref[g, c, row] = value[at : at + width]

    weight = weight_ref[lax.axis_index("space") % 2]
    conv_rows(rows_of(plane_ref, True), 1, weight, store, rows, lanes)
    for k in range(groups):
        outs[k][...] = all_ref[lax.rem(my_group() + k, groups)]


def unpack_kernel(swapped_ref, *refs):
    blocks, out_ref, rows_ref = refs[:-2], refs[-2], refs[-1]
    groups = len(blocks)
    _, rows, width, lanes = blocks[0].shape
    group, core = my_group(), my_core()
    for k in range(groups):
        source = lax.rem(group + groups - k, groups) * CORES
        rows_ref[source + core] = blocks[k][core]
        rows_ref[source + 1 - core] = swapped_ref[k]
    length = groups * CORES * rows
    turned = rows_ref[...].reshape(length, width, lanes).astype(F32)
    out_ref[:, 0] = jnp.swapaxes(turned, 0, 1).astype(BF16)


def arranged(weight):
    _, inner, outer = weight.shape
    taps = weight.reshape(3, 3, 3, inner, outer)
    own = taps[1].transpose(1, 3, 0, 2).reshape(3 * outer, 3 * inner)
    beside = taps[::2].transpose(0, 2, 4, 1, 3).reshape(2, 3 * outer, 3 * inner)
    return own, beside


def cost(rows, planes, full, lanes):
    flops = 2 * rows * lanes * full * full * 9 * planes
    return pl.CostEstimate(flops=flops, bytes_accessed=4_000_000, transcendentals=0)


def solution(mesh):
    space = mesh.shape["space"]
    chan = mesh.shape["chan"]
    groups = chan // CORES
    swap = [(i, i ^ 1) for i in range(chan)]

    near = [(i, i ^ 1) for i in range(space)]

    def far_partner(i, j):
        if i in (0, space - 1):
            return i * chan + (j ^ 1)
        return (((i - 1) ^ 1) + 1) * chan + j

    far = [(i * chan + j, far_partner(i, j)) for i in range(space) for j in range(chan)]

    order = sorted(range(1, groups), key=lambda k: abs(k - groups // 2))

    def ahead(k):
        return [(i, (i + CORES * k) % chan) for i in range(chan)]

    def call(kernel, shapes, inputs, scratch=(), **kwargs):
        single = not isinstance(shapes, list)
        return pl.pallas_call(
            kernel,
            out_shape=shapes,
            in_specs=[VMEM] * len(inputs),
            out_specs=VMEM if single else [VMEM] * len(shapes),
            scratch_shapes=scratch,
            compiler_params=PARAMS,
            **kwargs,
        )(*inputs)

    def per_device(volume, weight_one, bias_one, weight_two, bias_two):
        width, _, length, lanes = volume.shape
        full = width * chan
        rows = length // chan
        index = lax.axis_index("chan")
        group, core = index // CORES, index % CORES

        own_one, beside_one = arranged(weight_one)
        own_two, beside_two = arranged(weight_two)

        tall = CORES * rows + 2 * RIM
        pieces = call(
            pack_kernel,
            [jax.ShapeDtypeStruct((1, tall, width, lanes), BF16)] * groups,
            [volume],
            [pltpu.VMEM((length + 2 * RIM, width, lanes), BF16)],
            name="pack_rows",
        )
        kept = jnp.zeros((groups, tall, width, lanes), BF16)
        kept = lax.dynamic_update_slice_in_dim(kept, pieces[0], group, 0)
        for k in order:
            got = lax.ppermute(pieces[k], "chan", ahead(k))
            kept = lax.dynamic_update_slice_in_dim(kept, got, (group + groups - k) % groups, 0)

        def from_other_core(array, core):
            sent = lax.dynamic_slice_in_dim(array, (1 - core) * rows, rows + 2 * RIM, 1)
            return lax.ppermute(sent, "chan", swap)

        def halo(array):
            return lax.ppermute(array, ("space", "chan"), far), lax.ppermute(array, "space", near)

        partial = jax.ShapeDtypeStruct((rows + RIM, full, lanes), F32)
        joined = [pltpu.VMEM((rows + 2 * RIM, full, lanes), BF16)]
        work = cost(rows + RIM, 1, full, lanes)
        far_plane, near_plane = halo(kept)
        total, zero = call(
            first_own_kernel,
            [partial, jax.ShapeDtypeStruct((8, 128), jnp.int32)],
            [kept, from_other_core(kept, core), own_one, beside_one, bias_one[:, None]],
            joined,
            cost_estimate=work,
            name="first_own",
        )
        later_core = core + zero[0, 0]
        total = call(
            first_near_kernel,
            partial,
            [near_plane, from_other_core(near_plane, later_core), beside_one, total],
            joined,
            cost_estimate=work,
            name="first_near",
        )
        hidden = call(
            first_far_kernel,
            jax.ShapeDtypeStruct((rows + RIM, full, lanes), BF16),
            [far_plane, from_other_core(far_plane, later_core), beside_one, total, bias_one[:, None]],
            joined,
            cost_estimate=work,
            name="first_far",
        )

        partial = jax.ShapeDtypeStruct((rows, full, lanes), F32)
        work = cost(rows, 1, full, lanes)
        far_plane, near_plane = halo(hidden)
        total = call(own_kernel, partial, [hidden, own_two], cost_estimate=work, name="second_own")
        total = call(near_kernel, partial, [near_plane, beside_two, total], cost_estimate=work, name="second_near")
        blocks = call(
            second_kernel,
            [jax.ShapeDtypeStruct((CORES, rows, width, lanes), BF16)] * groups,
            [far_plane, beside_two, total, bias_two[:, None]],
            [pltpu.VMEM((groups, CORES, rows, width, lanes), BF16)],
            cost_estimate=work,
            name="second_far",
        )

        blocks = list(blocks)
        theirs = jnp.zeros((groups, rows, width, lanes), BF16)
        for k in [0, *order]:
            if k:
                blocks[k] = lax.ppermute(blocks[k], "chan", ahead(k))
            sent = lax.dynamic_index_in_dim(blocks[k], 1 - core, 0)
            theirs = lax.dynamic_update_slice_in_dim(theirs, sent, k, 0)
        swapped = lax.ppermute(theirs, "chan", swap)
        return call(
            unpack_kernel,
            jax.ShapeDtypeStruct(volume.shape, BF16),
            [swapped, *blocks],
            [pltpu.VMEM((chan, rows, width, lanes), BF16)],
            name="unpack_rows",
        )

    placed = (P("chan", "space", None, None), P(), P(), P(), P())
    return jax.shard_map(
        per_device,
        mesh=mesh,
        in_specs=placed,
        out_specs=P("chan", "space", None, None),
        check_vma=False,
    )
```

```python
import functools

import jax
import jax.numpy as jnp
from jax import lax
from jax.experimental import pallas as pl
from jax.experimental.pallas import tpu as pltpu
from jax.sharding import PartitionSpec as P

BF16 = jnp.bfloat16
F32 = jnp.float32
CORES = 2
RIM = 2
PARAMS = pltpu.CompilerParams(vmem_limit_bytes=24 * 1024 * 1024)
VMEM = pl.BlockSpec(memory_space=pltpu.VMEM)


def my_group():
    return lax.axis_index("chan") // CORES


def my_core():
    return lax.axis_index("chan") % CORES


def along_lanes(total, lanes):
    chans = total.shape[0] // 3
    lane = lax.broadcasted_iota(jnp.int32, (chans, lanes), 1)
    low = pltpu.roll(total[:chans], 1, 1)
    high = pltpu.roll(total[2 * chans :], lanes - 1, 1)
    return (
        total[chans : 2 * chans]
        + jnp.where(lane == 0, 0.0, low)
        + jnp.where(lane == lanes - 1, 0.0, high)
    )


def conv_rows(get, planes, weight, store, rows, lanes):
    for start in range(0, rows, 2):
        parts = []
        for a in range(planes):
            for e in range(3):
                pair = [get(a, start + e + n) for n in range(2)]
                parts.append(jnp.concatenate(pair, axis=1))
        stacked = jnp.concatenate(parts, axis=0)
        total = jnp.dot(weight, stacked, preferred_element_type=F32)
        for n in range(2):
            store(start + n, along_lanes(total[:, n * lanes : (n + 1) * lanes], lanes))


def pack_kernel(volume_ref, *refs):
    outs, rows_ref = refs[:-1], refs[-1]
    width, _, length, lanes = volume_ref.shape
    groups = len(outs)
    rows = length // groups
    edge = jnp.zeros((RIM, width, lanes), BF16)
    rows_ref[:RIM] = edge
    rows_ref[RIM + length :] = edge
    turned = jnp.swapaxes(volume_ref[:, 0].astype(F32), 0, 1)
    rows_ref[RIM : RIM + length] = turned.astype(BF16)
    for k in range(groups):
        target = lax.rem(my_group() + k, groups)
        outs[k][0] = rows_ref[pl.ds(target * rows, rows + 2 * RIM)]


def gather_rows(kept_ref, other_ref, joined_ref):
    core = my_core()
    groups, rows, width, lanes = other_ref.shape
    offset = core * (kept_ref.shape[1] - rows)
    for row in range(rows):
        parts = []
        for g in range(groups):
            kept = kept_ref[g, offset + row]
            other = other_ref[g, row]
            parts += [jnp.where(core == 0, kept, other), jnp.where(core == 0, other, kept)]
        joined_ref[row] = jnp.concatenate(parts, axis=0)


def rows_of(ref, masked):
    def get(_, row):
        value = ref[row]
        if masked:
            plane = lax.axis_index("space")
            edge = (plane == 0) | (plane == lax.axis_size("space") - 1)
            value = jnp.where(edge, jnp.zeros_like(value), value)
        return value

    return get


def own_kernel(plane_ref, weight_ref, out_ref):
    rows, _, lanes = out_ref.shape

    def store(row, value):
        out_ref[row] = value

    conv_rows(rows_of(plane_ref, False), 1, weight_ref[...], store, rows, lanes)


def near_kernel(plane_ref, weight_ref, before_ref, out_ref):
    rows, _, lanes = out_ref.shape

    def store(row, value):
        out_ref[row] = before_ref[row] + value

    weight = weight_ref[1 - lax.axis_index("space") % 2]
    conv_rows(rows_of(plane_ref, False), 1, weight, store, rows, lanes)


def first_own_kernel(kept_ref, other_ref, weight_ref, later_ref, bias_ref, out_ref, zero_ref, joined_ref):
    gather_rows(kept_ref, other_ref, joined_ref)
    own_kernel(joined_ref, weight_ref, out_ref)
    zero_ref[...] = jnp.zeros_like(zero_ref)


def first_near_kernel(kept_ref, other_ref, weight_ref, before_ref, out_ref, joined_ref):
    gather_rows(kept_ref, other_ref, joined_ref)
    near_kernel(joined_ref, weight_ref, before_ref, out_ref)


def first_far_kernel(kept_ref, other_ref, weight_ref, before_ref, bias_ref, out_ref, joined_ref):
    gather_rows(kept_ref, other_ref, joined_ref)
    rows, _, lanes = out_ref.shape
    block = lax.axis_index("chan")
    bias = bias_ref[...]

    def store(row, value):
        value = jnp.maximum(value + before_ref[row] + bias, 0.0)
        if row == 0:
            value = jnp.where(block == 0, 0.0, value)
        if row == rows - 1:
            value = jnp.where(block == lax.axis_size("chan") - 1, 0.0, value)
        out_ref[row] = value.astype(BF16)

    weight = weight_ref[lax.axis_index("space") % 2]
    conv_rows(rows_of(joined_ref, True), 1, weight, store, rows, lanes)


def second_kernel(plane_ref, weight_ref, before_ref, bias_ref, *refs):
    outs, all_ref = refs[:-1], refs[-1]
    groups, cores, rows, width, lanes = all_ref.shape
    bias = bias_ref[...]

    def store(row, value):
        value = jnp.maximum(value + before_ref[row] + bias, 0.0).astype(BF16)
        for g in range(groups):
            for c in range(cores):
                at = (g * cores + c) * width
                all_ref[g, c, row] = value[at : at + width]

    weight = weight_ref[lax.axis_index("space") % 2]
    conv_rows(rows_of(plane_ref, True), 1, weight, store, rows, lanes)
    for k in range(groups):
        outs[k][...] = all_ref[lax.rem(my_group() + k, groups)]


def unpack_kernel(order, early_ref, last_ref, *refs):
    blocks, out_ref, rows_ref = refs[:-2], refs[-2], refs[-1]
    groups = len(blocks)
    _, rows, width, lanes = blocks[0].shape
    group, core = my_group(), my_core()
    for i, k in enumerate(order):
        source = lax.rem(group + groups - k, groups) * CORES
        rows_ref[source + core] = blocks[k][core]
        rows_ref[source + 1 - core] = last_ref[0] if i == groups - 1 else early_ref[i]
    length = groups * CORES * rows
    turned = rows_ref[...].reshape(length, width, lanes).astype(F32)
    out_ref[:, 0] = jnp.swapaxes(turned, 0, 1).astype(BF16)


def arranged(weight):
    _, inner, outer = weight.shape
    taps = weight.reshape(3, 3, 3, inner, outer)
    own = taps[1].transpose(1, 3, 0, 2).reshape(3 * outer, 3 * inner)
    beside = taps[::2].transpose(0, 2, 4, 1, 3).reshape(2, 3 * outer, 3 * inner)
    return own, beside


def cost(rows, planes, full, lanes):
    flops = 2 * rows * lanes * full * full * 9 * planes
    return pl.CostEstimate(flops=flops, bytes_accessed=4_000_000, transcendentals=0)


def solution(mesh):
    space = mesh.shape["space"]
    chan = mesh.shape["chan"]
    groups = chan // CORES
    swap = [(i, i ^ 1) for i in range(chan)]

    near = [(i, i ^ 1) for i in range(space)]

    def far_partner(i, j):
        if i in (0, space - 1):
            return i * chan + (j ^ 1)
        return (((i - 1) ^ 1) + 1) * chan + j

    far = [(i * chan + j, far_partner(i, j)) for i in range(space) for j in range(chan)]

    order = sorted(range(1, groups), key=lambda k: abs(k - groups // 2))

    def ahead(k):
        return [(i, (i + CORES * k) % chan) for i in range(chan)]

    def call(kernel, shapes, inputs, scratch=(), **kwargs):
        single = not isinstance(shapes, list)
        return pl.pallas_call(
            kernel,
            out_shape=shapes,
            in_specs=[VMEM] * len(inputs),
            out_specs=VMEM if single else [VMEM] * len(shapes),
            scratch_shapes=scratch,
            compiler_params=PARAMS,
            **kwargs,
        )(*inputs)

    def per_device(volume, weight_one, bias_one, weight_two, bias_two):
        width, _, length, lanes = volume.shape
        full = width * chan
        rows = length // chan
        index = lax.axis_index("chan")
        group, core = index // CORES, index % CORES

        own_one, beside_one = arranged(weight_one)
        own_two, beside_two = arranged(weight_two)

        tall = CORES * rows + 2 * RIM
        pieces = call(
            pack_kernel,
            [jax.ShapeDtypeStruct((1, tall, width, lanes), BF16)] * groups,
            [volume],
            [pltpu.VMEM((length + 2 * RIM, width, lanes), BF16)],
            name="pack_rows",
        )
        kept = jnp.zeros((groups, tall, width, lanes), BF16)
        kept = lax.dynamic_update_slice_in_dim(kept, pieces[0], group, 0)
        for k in order:
            got = lax.ppermute(pieces[k], "chan", ahead(k))
            kept = lax.dynamic_update_slice_in_dim(kept, got, (group + groups - k) % groups, 0)

        def from_other_core(array, core):
            sent = lax.dynamic_slice_in_dim(array, (1 - core) * rows, rows + 2 * RIM, 1)
            return lax.ppermute(sent, "chan", swap)

        def halo(array):
            return lax.ppermute(array, ("space", "chan"), far), lax.ppermute(array, "space", near)

        partial = jax.ShapeDtypeStruct((rows + RIM, full, lanes), F32)
        joined = [pltpu.VMEM((rows + 2 * RIM, full, lanes), BF16)]
        work = cost(rows + RIM, 1, full, lanes)
        far_plane, near_plane = halo(kept)
        total, zero = call(
            first_own_kernel,
            [partial, jax.ShapeDtypeStruct((8, 128), jnp.int32)],
            [kept, from_other_core(kept, core), own_one, beside_one, bias_one[:, None]],
            joined,
            cost_estimate=work,
            name="first_own",
        )
        later_core = core + zero[0, 0]
        total = call(
            first_near_kernel,
            partial,
            [near_plane, from_other_core(near_plane, later_core), beside_one, total],
            joined,
            cost_estimate=work,
            name="first_near",
        )
        hidden = call(
            first_far_kernel,
            jax.ShapeDtypeStruct((rows + RIM, full, lanes), BF16),
            [far_plane, from_other_core(far_plane, later_core), beside_one, total, bias_one[:, None]],
            joined,
            cost_estimate=work,
            name="first_far",
        )

        partial = jax.ShapeDtypeStruct((rows, full, lanes), F32)
        work = cost(rows, 1, full, lanes)
        far_plane, near_plane = halo(hidden)
        total = call(own_kernel, partial, [hidden, own_two], cost_estimate=work, name="second_own")
        total = call(near_kernel, partial, [near_plane, beside_two, total], cost_estimate=work, name="second_near")
        blocks = call(
            second_kernel,
            [jax.ShapeDtypeStruct((CORES, rows, width, lanes), BF16)] * groups,
            [far_plane, beside_two, total, bias_two[:, None]],
            [pltpu.VMEM((groups, CORES, rows, width, lanes), BF16)],
            cost_estimate=work,
            name="second_far",
        )

        blocks = list(blocks)
        arrival = [0, *order]
        sent = []
        for k in arrival:
            if k:
                blocks[k] = lax.ppermute(blocks[k], "chan", ahead(k))
            sent.append(lax.dynamic_index_in_dim(blocks[k], 1 - core, 0))
        early = lax.ppermute(jnp.concatenate(sent[:-1]), "chan", swap)
        last = lax.ppermute(sent[-1], "chan", swap)
        return call(
            functools.partial(unpack_kernel, arrival),
            jax.ShapeDtypeStruct(volume.shape, BF16),
            [early, last, *blocks],
            [pltpu.VMEM((chan, rows, width, lanes), BF16)],
            name="unpack_rows",
        )

    placed = (P("chan", "space", None, None), P(), P(), P(), P())
    return jax.shard_map(
        per_device,
        mesh=mesh,
        in_specs=placed,
        out_specs=P("chan", "space", None, None),
        check_vma=False,
    )
```

```python
import jax
import jax.numpy as jnp
from jax import lax
from jax.experimental import pallas as pl
from jax.experimental.pallas import tpu as pltpu
from jax.sharding import PartitionSpec as P

BF16 = jnp.bfloat16
F32 = jnp.float32
CORES = 2
RIM = 2
PARAMS = pltpu.CompilerParams(vmem_limit_bytes=24 * 1024 * 1024)
VMEM = pl.BlockSpec(memory_space=pltpu.VMEM)


def my_group():
    return lax.axis_index("chan") // CORES


def my_core():
    return lax.axis_index("chan") % CORES


def along_lanes(total, lanes):
    chans = total.shape[0] // 3
    lane = lax.broadcasted_iota(jnp.int32, (chans, lanes), 1)
    low = pltpu.roll(total[:chans], 1, 1)
    high = pltpu.roll(total[2 * chans :], lanes - 1, 1)
    return (
        total[chans : 2 * chans]
        + jnp.where(lane == 0, 0.0, low)
        + jnp.where(lane == lanes - 1, 0.0, high)
    )


def conv_rows(get, planes, weight, store, rows, lanes):
    for start in range(0, rows, 2):
        parts = []
        for a in range(planes):
            for e in range(3):
                pair = [get(a, start + e + n) for n in range(2)]
                parts.append(jnp.concatenate(pair, axis=1))
        stacked = jnp.concatenate(parts, axis=0)
        total = jnp.dot(weight, stacked, preferred_element_type=F32)
        for n in range(2):
            store(start + n, along_lanes(total[:, n * lanes : (n + 1) * lanes], lanes))


def pack_kernel(volume_ref, *refs):
    outs, rows_ref = refs[:-1], refs[-1]
    width, _, length, lanes = volume_ref.shape
    groups = len(outs)
    rows = length // groups
    edge = jnp.zeros((RIM, width, lanes), BF16)
    rows_ref[:RIM] = edge
    rows_ref[RIM + length :] = edge
    turned = jnp.swapaxes(volume_ref[:, 0].astype(F32), 0, 1)
    rows_ref[RIM : RIM + length] = turned.astype(BF16)
    for k in range(groups):
        target = lax.rem(my_group() + k, groups)
        outs[k][0] = rows_ref[pl.ds(target * rows, rows + 2 * RIM)]


def gather_rows(kept_ref, other_ref, joined_ref):
    core = my_core()
    groups, rows, width, lanes = other_ref.shape
    offset = core * (kept_ref.shape[1] - rows)
    for row in range(rows):
        parts = []
        for g in range(groups):
            kept = kept_ref[g, offset + row]
            other = other_ref[g, row]
            parts += [jnp.where(core == 0, kept, other), jnp.where(core == 0, other, kept)]
        joined_ref[row] = jnp.concatenate(parts, axis=0)


def rows_of(ref, masked):
    def get(_, row):
        value = ref[row]
        if masked:
            plane = lax.axis_index("space")
            edge = (plane == 0) | (plane == lax.axis_size("space") - 1)
            value = jnp.where(edge, jnp.zeros_like(value), value)
        return value

    return get


def own_kernel(plane_ref, weight_ref, out_ref):
    rows, _, lanes = out_ref.shape

    def store(row, value):
        out_ref[row] = value

    conv_rows(rows_of(plane_ref, False), 1, weight_ref[...], store, rows, lanes)


def near_kernel(plane_ref, weight_ref, before_ref, out_ref):
    rows, _, lanes = out_ref.shape

    def store(row, value):
        out_ref[row] = before_ref[row] + value

    weight = weight_ref[1 - lax.axis_index("space") % 2]
    conv_rows(rows_of(plane_ref, False), 1, weight, store, rows, lanes)


def first_own_kernel(kept_ref, other_ref, weight_ref, later_ref, bias_ref, out_ref, zero_ref, joined_ref):
    gather_rows(kept_ref, other_ref, joined_ref)
    own_kernel(joined_ref, weight_ref, out_ref)
    zero_ref[...] = jnp.zeros_like(zero_ref)


def first_near_kernel(kept_ref, other_ref, weight_ref, before_ref, out_ref, zero_ref, joined_ref):
    zero_ref[...] = jnp.zeros_like(zero_ref)
    gather_rows(kept_ref, other_ref, joined_ref)
    near_kernel(joined_ref, weight_ref, before_ref, out_ref)


def first_far_kernel(kept_ref, other_ref, weight_ref, before_ref, bias_ref, out_ref, joined_ref):
    gather_rows(kept_ref, other_ref, joined_ref)
    rows, _, lanes = out_ref.shape
    block = lax.axis_index("chan")
    bias = bias_ref[...]

    def store(row, value):
        value = jnp.maximum(value + before_ref[row] + bias, 0.0)
        if row == 0:
            value = jnp.where(block == 0, 0.0, value)
        if row == rows - 1:
            value = jnp.where(block == lax.axis_size("chan") - 1, 0.0, value)
        out_ref[row] = value.astype(BF16)

    weight = weight_ref[lax.axis_index("space") % 2]
    conv_rows(rows_of(joined_ref, True), 1, weight, store, rows, lanes)


def second_kernel(plane_ref, weight_ref, before_ref, bias_ref, *refs):
    outs, all_ref = refs[:-1], refs[-1]
    groups, cores, rows, width, lanes = all_ref.shape
    bias = bias_ref[...]

    def store(row, value):
        value = jnp.maximum(value + before_ref[row] + bias, 0.0).astype(BF16)
        for g in range(groups):
            for c in range(cores):
                at = (g * cores + c) * width
                all_ref[g, c, row] = value[at : at + width]

    weight = weight_ref[lax.axis_index("space") % 2]
    conv_rows(rows_of(plane_ref, True), 1, weight, store, rows, lanes)
    for k in range(groups):
        outs[k][...] = all_ref[lax.rem(my_group() + k, groups)]


def unpack_kernel(swapped_ref, *refs):
    blocks, out_ref, rows_ref = refs[:-2], refs[-2], refs[-1]
    groups = len(blocks)
    _, rows, width, lanes = blocks[0].shape
    group, core = my_group(), my_core()
    for k in range(groups):
        source = lax.rem(group + groups - k, groups) * CORES
        rows_ref[source + core] = blocks[k][core]
        rows_ref[source + 1 - core] = swapped_ref[k]
    length = groups * CORES * rows
    turned = rows_ref[...].reshape(length, width, lanes).astype(F32)
    out_ref[:, 0] = jnp.swapaxes(turned, 0, 1).astype(BF16)


def arranged(weight):
    _, inner, outer = weight.shape
    taps = weight.reshape(3, 3, 3, inner, outer)
    own = taps[1].transpose(1, 3, 0, 2).reshape(3 * outer, 3 * inner)
    beside = taps[::2].transpose(0, 2, 4, 1, 3).reshape(2, 3 * outer, 3 * inner)
    return own, beside


def cost(rows, planes, full, lanes):
    flops = 2 * rows * lanes * full * full * 9 * planes
    return pl.CostEstimate(flops=flops, bytes_accessed=4_000_000, transcendentals=0)


def solution(mesh):
    space = mesh.shape["space"]
    chan = mesh.shape["chan"]
    groups = chan // CORES
    swap = [(i, i ^ 1) for i in range(chan)]

    near = [(i, i ^ 1) for i in range(space)]

    def far_partner(i, j):
        if i in (0, space - 1):
            return i * chan + (j ^ 1)
        return (((i - 1) ^ 1) + 1) * chan + j

    far = [(i * chan + j, far_partner(i, j)) for i in range(space) for j in range(chan)]

    order = sorted(range(1, groups), key=lambda k: abs(k - groups // 2))

    def ahead(k):
        return [(i, (i + CORES * k) % chan) for i in range(chan)]

    def call(kernel, shapes, inputs, scratch=(), **kwargs):
        single = not isinstance(shapes, list)
        return pl.pallas_call(
            kernel,
            out_shape=shapes,
            in_specs=[VMEM] * len(inputs),
            out_specs=VMEM if single else [VMEM] * len(shapes),
            scratch_shapes=scratch,
            compiler_params=PARAMS,
            **kwargs,
        )(*inputs)

    def per_device(volume, weight_one, bias_one, weight_two, bias_two):
        width, _, length, lanes = volume.shape
        full = width * chan
        rows = length // chan
        index = lax.axis_index("chan")
        group, core = index // CORES, index % CORES

        own_one, beside_one = arranged(weight_one)
        own_two, beside_two = arranged(weight_two)

        tall = CORES * rows + 2 * RIM
        pieces = call(
            pack_kernel,
            [jax.ShapeDtypeStruct((1, tall, width, lanes), BF16)] * groups,
            [volume],
            [pltpu.VMEM((length + 2 * RIM, width, lanes), BF16)],
            name="pack_rows",
        )
        kept = jnp.zeros((groups, tall, width, lanes), BF16)
        kept = lax.dynamic_update_slice_in_dim(kept, pieces[0], group, 0)
        for k in order:
            got = lax.ppermute(pieces[k], "chan", ahead(k))
            kept = lax.dynamic_update_slice_in_dim(kept, got, (group + groups - k) % groups, 0)

        def from_other_core(array, core):
            sent = lax.dynamic_slice_in_dim(array, (1 - core) * rows, rows + 2 * RIM, 1)
            return lax.ppermute(sent, "chan", swap)

        def halo(array):
            return lax.ppermute(array, ("space", "chan"), far), lax.ppermute(array, "space", near)

        partial = jax.ShapeDtypeStruct((rows + RIM, full, lanes), F32)
        joined = [pltpu.VMEM((rows + 2 * RIM, full, lanes), BF16)]
        work = cost(rows + RIM, 1, full, lanes)
        far_plane, near_plane = halo(kept)
        total, zero = call(
            first_own_kernel,
            [partial, jax.ShapeDtypeStruct((8, 128), jnp.int32)],
            [kept, from_other_core(kept, core), own_one, beside_one, bias_one[:, None]],
            joined,
            cost_estimate=work,
            name="first_own",
        )
        later_core = core + zero[0, 0]
        total, zero = call(
            first_near_kernel,
            [partial, jax.ShapeDtypeStruct((8, 128), jnp.int32)],
            [near_plane, from_other_core(near_plane, later_core), beside_one, total],
            joined,
            cost_estimate=work,
            name="first_near",
        )
        later_core = core + zero[0, 0]
        hidden = call(
            first_far_kernel,
            jax.ShapeDtypeStruct((rows + RIM, full, lanes), BF16),
            [far_plane, from_other_core(far_plane, later_core), beside_one, total, bias_one[:, None]],
            joined,
            cost_estimate=work,
            name="first_far",
        )

        partial = jax.ShapeDtypeStruct((rows, full, lanes), F32)
        work = cost(rows, 1, full, lanes)
        far_plane, near_plane = halo(hidden)
        total = call(own_kernel, partial, [hidden, own_two], cost_estimate=work, name="second_own")
        total = call(near_kernel, partial, [near_plane, beside_two, total], cost_estimate=work, name="second_near")
        blocks = call(
            second_kernel,
            [jax.ShapeDtypeStruct((CORES, rows, width, lanes), BF16)] * groups,
            [far_plane, beside_two, total, bias_two[:, None]],
            [pltpu.VMEM((groups, CORES, rows, width, lanes), BF16)],
            cost_estimate=work,
            name="second_far",
        )

        blocks = list(blocks)
        theirs = jnp.zeros((groups, rows, width, lanes), BF16)
        for k in [0, *order]:
            if k:
                blocks[k] = lax.ppermute(blocks[k], "chan", ahead(k))
            sent = lax.dynamic_index_in_dim(blocks[k], 1 - core, 0)
            theirs = lax.dynamic_update_slice_in_dim(theirs, sent, k, 0)
        swapped = lax.ppermute(theirs, "chan", swap)
        return call(
            unpack_kernel,
            jax.ShapeDtypeStruct(volume.shape, BF16),
            [swapped, *blocks],
            [pltpu.VMEM((chan, rows, width, lanes), BF16)],
            name="unpack_rows",
        )

    placed = (P("chan", "space", None, None), P(), P(), P(), P())
    return jax.shard_map(
        per_device,
        mesh=mesh,
        in_specs=placed,
        out_specs=P("chan", "space", None, None),
        check_vma=False,
    )
```

```python
import jax
import jax.numpy as jnp
from jax import lax
from jax.experimental import pallas as pl
from jax.experimental.pallas import tpu as pltpu
from jax.sharding import PartitionSpec as P

BF16 = jnp.bfloat16
F32 = jnp.float32
CORES = 2
RIM = 2
PARAMS = pltpu.CompilerParams(vmem_limit_bytes=24 * 1024 * 1024)
VMEM = pl.BlockSpec(memory_space=pltpu.VMEM)


def my_group():
    return lax.axis_index("chan") // CORES


def my_core():
    return lax.axis_index("chan") % CORES


def along_lanes(total, lanes):
    chans = total.shape[0] // 3
    lane = lax.broadcasted_iota(jnp.int32, (chans, lanes), 1)
    low = pltpu.roll(total[:chans], 1, 1)
    high = pltpu.roll(total[2 * chans :], lanes - 1, 1)
    return (
        total[chans : 2 * chans]
        + jnp.where(lane == 0, 0.0, low)
        + jnp.where(lane == lanes - 1, 0.0, high)
    )


def conv_rows(get, planes, weight, store, rows, lanes):
    for start in range(0, rows, 2):
        parts = []
        for a in range(planes):
            for e in range(3):
                pair = [get(a, start + e + n) for n in range(2)]
                parts.append(jnp.concatenate(pair, axis=1))
        stacked = jnp.concatenate(parts, axis=0)
        total = jnp.dot(weight, stacked, preferred_element_type=F32)
        for n in range(2):
            store(start + n, along_lanes(total[:, n * lanes : (n + 1) * lanes], lanes))


def pack_kernel(volume_ref, *refs):
    outs, rows_ref = refs[:-1], refs[-1]
    width, _, length, lanes = volume_ref.shape
    groups = len(outs)
    rows = length // groups
    edge = jnp.zeros((RIM, width, lanes), BF16)
    rows_ref[:RIM] = edge
    rows_ref[RIM + length :] = edge
    turned = jnp.swapaxes(volume_ref[:, 0].astype(F32), 0, 1)
    rows_ref[RIM : RIM + length] = turned.astype(BF16)
    for k in range(groups):
        target = lax.rem(my_group() + k, groups)
        outs[k][0] = rows_ref[pl.ds(target * rows, rows + 2 * RIM)]


def gather_rows(kept_ref, other_ref, joined_ref):
    core = my_core()
    groups, rows, width, lanes = other_ref.shape
    offset = core * (kept_ref.shape[1] - rows)
    for row in range(rows):
        parts = []
        for g in range(groups):
            kept = kept_ref[g, offset + row]
            other = other_ref[g, row]
            parts += [jnp.where(core == 0, kept, other), jnp.where(core == 0, other, kept)]
        joined_ref[row] = jnp.concatenate(parts, axis=0)


def rows_of(ref, masked):
    def get(_, row):
        value = ref[row]
        if masked:
            plane = lax.axis_index("space")
            edge = (plane == 0) | (plane == lax.axis_size("space") - 1)
            value = jnp.where(edge, jnp.zeros_like(value), value)
        return value

    return get


def own_kernel(plane_ref, weight_ref, out_ref):
    rows, _, lanes = out_ref.shape

    def store(row, value):
        out_ref[row] = value

    conv_rows(rows_of(plane_ref, False), 1, weight_ref[...], store, rows, lanes)


def near_kernel(plane_ref, weight_ref, before_ref, out_ref):
    rows, _, lanes = out_ref.shape

    def store(row, value):
        out_ref[row] = before_ref[row] + value

    weight = weight_ref[1 - lax.axis_index("space") % 2]
    conv_rows(rows_of(plane_ref, False), 1, weight, store, rows, lanes)


def first_own_kernel(kept_ref, other_ref, weight_ref, later_ref, bias_ref, out_ref, zero_ref, joined_ref):
    gather_rows(kept_ref, other_ref, joined_ref)
    own_kernel(joined_ref, weight_ref, out_ref)
    zero_ref[...] = jnp.zeros_like(zero_ref)


def first_near_kernel(kept_ref, other_ref, weight_ref, before_ref, out_ref, joined_ref):
    gather_rows(kept_ref, other_ref, joined_ref)
    near_kernel(joined_ref, weight_ref, before_ref, out_ref)


def first_far_kernel(kept_ref, other_ref, weight_ref, before_ref, bias_ref, out_ref, joined_ref):
    gather_rows(kept_ref, other_ref, joined_ref)
    rows, _, lanes = out_ref.shape
    block = lax.axis_index("chan")
    bias = bias_ref[...]

    def store(row, value):
        value = jnp.maximum(value + before_ref[row] + bias, 0.0)
        if row == 0:
            value = jnp.where(block == 0, 0.0, value)
        if row == rows - 1:
            value = jnp.where(block == lax.axis_size("chan") - 1, 0.0, value)
        out_ref[row] = value.astype(BF16)

    weight = weight_ref[lax.axis_index("space") % 2]
    conv_rows(rows_of(joined_ref, True), 1, weight, store, rows, lanes)


def second_kernel(plane_ref, weight_ref, before_ref, bias_ref, *refs):
    outs, all_ref = refs[:-1], refs[-1]
    groups, cores, rows, width, lanes = all_ref.shape
    bias = bias_ref[...]

    def store(row, value):
        value = jnp.maximum(value + before_ref[row] + bias, 0.0).astype(BF16)
        for g in range(groups):
            for c in range(cores):
                at = (g * cores + c) * width
                all_ref[g, c, row] = value[at : at + width]

    weight = weight_ref[lax.axis_index("space") % 2]
    conv_rows(rows_of(plane_ref, True), 1, weight, store, rows, lanes)
    for k in range(groups):
        outs[k][...] = all_ref[lax.rem(my_group() + k, groups)]


def unpack_kernel(swapped_ref, *refs):
    blocks, out_ref, rows_ref = refs[:-2], refs[-2], refs[-1]
    groups = len(blocks)
    _, rows, width, lanes = blocks[0].shape
    group, core = my_group(), my_core()
    for k in range(groups):
        source = lax.rem(group + groups - k, groups) * CORES
        rows_ref[source + core] = blocks[k][core]
        rows_ref[source + 1 - core] = swapped_ref[k]
    length = groups * CORES * rows
    turned = rows_ref[...].reshape(length, width, lanes).astype(F32)
    out_ref[:, 0] = jnp.swapaxes(turned, 0, 1).astype(BF16)


def arranged(weight):
    _, inner, outer = weight.shape
    taps = weight.reshape(3, 3, 3, inner, outer)
    own = taps[1].transpose(1, 3, 0, 2).reshape(3 * outer, 3 * inner)
    beside = taps[::2].transpose(0, 2, 4, 1, 3).reshape(2, 3 * outer, 3 * inner)
    return own, beside


def cost(rows, planes, full, lanes):
    flops = 2 * rows * lanes * full * full * 9 * planes
    return pl.CostEstimate(flops=flops, bytes_accessed=4_000_000, transcendentals=0)


def solution(mesh):
    space = mesh.shape["space"]
    chan = mesh.shape["chan"]
    groups = chan // CORES
    swap = [(i, i ^ 1) for i in range(chan)]

    near = [(i, i ^ 1) for i in range(space)]

    def far_partner(i, j):
        if i in (0, space - 1):
            return i * chan + (j ^ 1)
        return (((i - 1) ^ 1) + 1) * chan + j

    far = [(i * chan + j, far_partner(i, j)) for i in range(space) for j in range(chan)]

    order = sorted(range(1, groups), key=lambda k: (abs(k - groups // 2), -k))

    def ahead(k):
        return [(i, (i + CORES * k) % chan) for i in range(chan)]

    def call(kernel, shapes, inputs, scratch=(), **kwargs):
        single = not isinstance(shapes, list)
        return pl.pallas_call(
            kernel,
            out_shape=shapes,
            in_specs=[VMEM] * len(inputs),
            out_specs=VMEM if single else [VMEM] * len(shapes),
            scratch_shapes=scratch,
            compiler_params=PARAMS,
            **kwargs,
        )(*inputs)

    def per_device(volume, weight_one, bias_one, weight_two, bias_two):
        width, _, length, lanes = volume.shape
        full = width * chan
        rows = length // chan
        index = lax.axis_index("chan")
        group, core = index // CORES, index % CORES

        own_one, beside_one = arranged(weight_one)
        own_two, beside_two = arranged(weight_two)

        tall = CORES * rows + 2 * RIM
        pieces = call(
            pack_kernel,
            [jax.ShapeDtypeStruct((1, tall, width, lanes), BF16)] * groups,
            [volume],
            [pltpu.VMEM((length + 2 * RIM, width, lanes), BF16)],
            name="pack_rows",
        )
        kept = jnp.zeros((groups, tall, width, lanes), BF16)
        kept = lax.dynamic_update_slice_in_dim(kept, pieces[0], group, 0)
        for k in order:
            got = lax.ppermute(pieces[k], "chan", ahead(k))
            kept = lax.dynamic_update_slice_in_dim(kept, got, (group + groups - k) % groups, 0)

        def from_other_core(array, core):
            sent = lax.dynamic_slice_in_dim(array, (1 - core) * rows, rows + 2 * RIM, 1)
            return lax.ppermute(sent, "chan", swap)

        def halo(array):
            return lax.ppermute(array, ("space", "chan"), far), lax.ppermute(array, "space", near)

        partial = jax.ShapeDtypeStruct((rows + RIM, full, lanes), F32)
        joined = [pltpu.VMEM((rows + 2 * RIM, full, lanes), BF16)]
        work = cost(rows + RIM, 1, full, lanes)
        far_plane, near_plane = halo(kept)
        total, zero = call(
            first_own_kernel,
            [partial, jax.ShapeDtypeStruct((8, 128), jnp.int32)],
            [kept, from_other_core(kept, core), own_one, beside_one, bias_one[:, None]],
            joined,
            cost_estimate=work,
            name="first_own",
        )
        later_core = core + zero[0, 0]
        total = call(
            first_near_kernel,
            partial,
            [near_plane, from_other_core(near_plane, later_core), beside_one, total],
            joined,
            cost_estimate=work,
            name="first_near",
        )
        hidden = call(
            first_far_kernel,
            jax.ShapeDtypeStruct((rows + RIM, full, lanes), BF16),
            [far_plane, from_other_core(far_plane, later_core), beside_one, total, bias_one[:, None]],
            joined,
            cost_estimate=work,
            name="first_far",
        )

        partial = jax.ShapeDtypeStruct((rows, full, lanes), F32)
        work = cost(rows, 1, full, lanes)
        far_plane, near_plane = halo(hidden)
        total = call(own_kernel, partial, [hidden, own_two], cost_estimate=work, name="second_own")
        total = call(near_kernel, partial, [near_plane, beside_two, total], cost_estimate=work, name="second_near")
        blocks = call(
            second_kernel,
            [jax.ShapeDtypeStruct((CORES, rows, width, lanes), BF16)] * groups,
            [far_plane, beside_two, total, bias_two[:, None]],
            [pltpu.VMEM((groups, CORES, rows, width, lanes), BF16)],
            cost_estimate=work,
            name="second_far",
        )

        blocks = list(blocks)
        theirs = jnp.zeros((groups, rows, width, lanes), BF16)
        for k in [0, *order]:
            if k:
                blocks[k] = lax.ppermute(blocks[k], "chan", ahead(k))
            sent = lax.dynamic_index_in_dim(blocks[k], 1 - core, 0)
            theirs = lax.dynamic_update_slice_in_dim(theirs, sent, k, 0)
        swapped = lax.ppermute(theirs, "chan", swap)
        return call(
            unpack_kernel,
            jax.ShapeDtypeStruct(volume.shape, BF16),
            [swapped, *blocks],
            [pltpu.VMEM((chan, rows, width, lanes), BF16)],
            name="unpack_rows",
        )

    placed = (P("chan", "space", None, None), P(), P(), P(), P())
    return jax.shard_map(
        per_device,
        mesh=mesh,
        in_specs=placed,
        out_specs=P("chan", "space", None, None),
        check_vma=False,
    )
```

```python
import functools

import jax
import jax.numpy as jnp
from jax import lax
from jax.experimental import pallas as pl
from jax.experimental.pallas import tpu as pltpu
from jax.sharding import PartitionSpec as P

BF16 = jnp.bfloat16
F32 = jnp.float32
CORES = 2
RIM = 2
PARAMS = pltpu.CompilerParams(vmem_limit_bytes=24 * 1024 * 1024)
VMEM = pl.BlockSpec(memory_space=pltpu.VMEM)


def my_group():
    return lax.axis_index("chan") // CORES


def my_core():
    return lax.axis_index("chan") % CORES


def along_lanes(total, lanes):
    chans = total.shape[0] // 3
    lane = lax.broadcasted_iota(jnp.int32, (chans, lanes), 1)
    low = pltpu.roll(total[:chans], 1, 1)
    high = pltpu.roll(total[2 * chans :], lanes - 1, 1)
    return (
        total[chans : 2 * chans]
        + jnp.where(lane == 0, 0.0, low)
        + jnp.where(lane == lanes - 1, 0.0, high)
    )


def conv_rows(get, planes, weight, store, rows, lanes):
    for start in range(0, rows, 2):
        parts = []
        for a in range(planes):
            for e in range(3):
                pair = [get(a, start + e + n) for n in range(2)]
                parts.append(jnp.concatenate(pair, axis=1))
        stacked = jnp.concatenate(parts, axis=0)
        total = jnp.dot(weight, stacked, preferred_element_type=F32)
        for n in range(2):
            store(start + n, along_lanes(total[:, n * lanes : (n + 1) * lanes], lanes))


def pack_kernel(volume_ref, *refs):
    outs, rows_ref = refs[:-1], refs[-1]
    width, _, length, lanes = volume_ref.shape
    groups = len(outs)
    rows = length // groups
    edge = jnp.zeros((RIM, width, lanes), BF16)
    rows_ref[:RIM] = edge
    rows_ref[RIM + length :] = edge
    turned = jnp.swapaxes(volume_ref[:, 0].astype(F32), 0, 1)
    rows_ref[RIM : RIM + length] = turned.astype(BF16)
    for k in range(groups):
        target = lax.rem(my_group() + k, groups)
        outs[k][0] = rows_ref[pl.ds(target * rows, rows + 2 * RIM)]


def gather_rows(kept_ref, other_ref, joined_ref):
    core = my_core()
    groups, rows, width, lanes = other_ref.shape
    offset = core * (kept_ref.shape[1] - rows)
    for row in range(rows):
        parts = []
        for g in range(groups):
            kept = kept_ref[g, offset + row]
            other = other_ref[g, row]
            parts += [jnp.where(core == 0, kept, other), jnp.where(core == 0, other, kept)]
        joined_ref[row] = jnp.concatenate(parts, axis=0)


def rows_of(ref, masked):
    def get(_, row):
        value = ref[row]
        if masked:
            plane = lax.axis_index("space")
            edge = (plane == 0) | (plane == lax.axis_size("space") - 1)
            value = jnp.where(edge, jnp.zeros_like(value), value)
        return value

    return get


def own_kernel(plane_ref, weight_ref, out_ref):
    rows, _, lanes = out_ref.shape

    def store(row, value):
        out_ref[row] = value

    conv_rows(rows_of(plane_ref, False), 1, weight_ref[...], store, rows, lanes)


def near_kernel(plane_ref, weight_ref, before_ref, out_ref):
    rows, _, lanes = out_ref.shape

    def store(row, value):
        out_ref[row] = before_ref[row] + value

    weight = weight_ref[1 - lax.axis_index("space") % 2]
    conv_rows(rows_of(plane_ref, False), 1, weight, store, rows, lanes)


def first_own_kernel(kept_ref, other_ref, weight_ref, later_ref, bias_ref, out_ref, zero_ref, joined_ref):
    gather_rows(kept_ref, other_ref, joined_ref)
    own_kernel(joined_ref, weight_ref, out_ref)
    zero_ref[...] = jnp.zeros_like(zero_ref)


def first_near_kernel(kept_ref, other_ref, weight_ref, before_ref, out_ref, joined_ref):
    gather_rows(kept_ref, other_ref, joined_ref)
    near_kernel(joined_ref, weight_ref, before_ref, out_ref)


def first_far_kernel(kept_ref, other_ref, weight_ref, before_ref, bias_ref, out_ref, joined_ref):
    gather_rows(kept_ref, other_ref, joined_ref)
    rows, _, lanes = out_ref.shape
    block = lax.axis_index("chan")
    bias = bias_ref[...]

    def store(row, value):
        value = jnp.maximum(value + before_ref[row] + bias, 0.0)
        if row == 0:
            value = jnp.where(block == 0, 0.0, value)
        if row == rows - 1:
            value = jnp.where(block == lax.axis_size("chan") - 1, 0.0, value)
        out_ref[row] = value.astype(BF16)

    weight = weight_ref[lax.axis_index("space") % 2]
    conv_rows(rows_of(joined_ref, True), 1, weight, store, rows, lanes)


def second_kernel(plane_ref, weight_ref, before_ref, bias_ref, *refs):
    outs, all_ref = refs[:-1], refs[-1]
    groups, cores, rows, width, lanes = all_ref.shape
    bias = bias_ref[...]

    def store(row, value):
        value = jnp.maximum(value + before_ref[row] + bias, 0.0).astype(BF16)
        for g in range(groups):
            for c in range(cores):
                at = (g * cores + c) * width
                all_ref[g, c, row] = value[at : at + width]

    weight = weight_ref[lax.axis_index("space") % 2]
    conv_rows(rows_of(plane_ref, True), 1, weight, store, rows, lanes)
    for k in range(groups):
        outs[k][...] = all_ref[lax.rem(my_group() + k, groups)]


def unpack_kernel(order, early_ref, last_ref, *refs):
    blocks, out_ref, rows_ref = refs[:-2], refs[-2], refs[-1]
    groups = len(blocks)
    _, rows, width, lanes = blocks[0].shape
    group, core = my_group(), my_core()
    for i, k in enumerate(order):
        source = lax.rem(group + groups - k, groups) * CORES
        rows_ref[source + core] = blocks[k][core]
        rows_ref[source + 1 - core] = last_ref[0] if i == groups - 1 else early_ref[i]
    length = groups * CORES * rows
    turned = rows_ref[...].reshape(length, width, lanes).astype(F32)
    out_ref[:, 0] = jnp.swapaxes(turned, 0, 1).astype(BF16)


def arranged(weight):
    _, inner, outer = weight.shape
    taps = weight.reshape(3, 3, 3, inner, outer)
    own = taps[1].transpose(1, 3, 0, 2).reshape(3 * outer, 3 * inner)
    beside = taps[::2].transpose(0, 2, 4, 1, 3).reshape(2, 3 * outer, 3 * inner)
    return own, beside


def cost(rows, planes, full, lanes):
    flops = 2 * rows * lanes * full * full * 9 * planes
    return pl.CostEstimate(flops=flops, bytes_accessed=4_000_000, transcendentals=0)


def solution(mesh):
    space = mesh.shape["space"]
    chan = mesh.shape["chan"]
    groups = chan // CORES
    swap = [(i, i ^ 1) for i in range(chan)]

    near = [(i, i ^ 1) for i in range(space)]

    def far_partner(i, j):
        if i in (0, space - 1):
            return i * chan + (j ^ 1)
        return (((i - 1) ^ 1) + 1) * chan + j

    far = [(i * chan + j, far_partner(i, j)) for i in range(space) for j in range(chan)]

    order = sorted(range(1, groups), key=lambda k: (abs(k - groups // 2), -k))

    def ahead(k):
        return [(i, (i + CORES * k) % chan) for i in range(chan)]

    def call(kernel, shapes, inputs, scratch=(), **kwargs):
        single = not isinstance(shapes, list)
        return pl.pallas_call(
            kernel,
            out_shape=shapes,
            in_specs=[VMEM] * len(inputs),
            out_specs=VMEM if single else [VMEM] * len(shapes),
            scratch_shapes=scratch,
            compiler_params=PARAMS,
            **kwargs,
        )(*inputs)

    def per_device(volume, weight_one, bias_one, weight_two, bias_two):
        width, _, length, lanes = volume.shape
        full = width * chan
        rows = length // chan
        index = lax.axis_index("chan")
        group, core = index // CORES, index % CORES

        own_one, beside_one = arranged(weight_one)
        own_two, beside_two = arranged(weight_two)

        tall = CORES * rows + 2 * RIM
        pieces = call(
            pack_kernel,
            [jax.ShapeDtypeStruct((1, tall, width, lanes), BF16)] * groups,
            [volume],
            [pltpu.VMEM((length + 2 * RIM, width, lanes), BF16)],
            name="pack_rows",
        )
        kept = jnp.zeros((groups, tall, width, lanes), BF16)
        kept = lax.dynamic_update_slice_in_dim(kept, pieces[0], group, 0)
        for k in order:
            got = lax.ppermute(pieces[k], "chan", ahead(k))
            kept = lax.dynamic_update_slice_in_dim(kept, got, (group + groups - k) % groups, 0)

        def from_other_core(array, core):
            sent = lax.dynamic_slice_in_dim(array, (1 - core) * rows, rows + 2 * RIM, 1)
            return lax.ppermute(sent, "chan", swap)

        def halo(array):
            return lax.ppermute(array, ("space", "chan"), far), lax.ppermute(array, "space", near)

        partial = jax.ShapeDtypeStruct((rows + RIM, full, lanes), F32)
        joined = [pltpu.VMEM((rows + 2 * RIM, full, lanes), BF16)]
        work = cost(rows + RIM, 1, full, lanes)
        far_plane, near_plane = halo(kept)
        total, zero = call(
            first_own_kernel,
            [partial, jax.ShapeDtypeStruct((8, 128), jnp.int32)],
            [kept, from_other_core(kept, core), own_one, beside_one, bias_one[:, None]],
            joined,
            cost_estimate=work,
            name="first_own",
        )
        later_core = core + zero[0, 0]
        total = call(
            first_near_kernel,
            partial,
            [near_plane, from_other_core(near_plane, later_core), beside_one, total],
            joined,
            cost_estimate=work,
            name="first_near",
        )
        hidden = call(
            first_far_kernel,
            jax.ShapeDtypeStruct((rows + RIM, full, lanes), BF16),
            [far_plane, from_other_core(far_plane, later_core), beside_one, total, bias_one[:, None]],
            joined,
            cost_estimate=work,
            name="first_far",
        )

        partial = jax.ShapeDtypeStruct((rows, full, lanes), F32)
        work = cost(rows, 1, full, lanes)
        far_plane, near_plane = halo(hidden)
        total = call(own_kernel, partial, [hidden, own_two], cost_estimate=work, name="second_own")
        total = call(near_kernel, partial, [near_plane, beside_two, total], cost_estimate=work, name="second_near")
        blocks = call(
            second_kernel,
            [jax.ShapeDtypeStruct((CORES, rows, width, lanes), BF16)] * groups,
            [far_plane, beside_two, total, bias_two[:, None]],
            [pltpu.VMEM((groups, CORES, rows, width, lanes), BF16)],
            cost_estimate=work,
            name="second_far",
        )

        blocks = list(blocks)
        arrival = [0, *order]
        sent = []
        for k in arrival:
            if k:
                blocks[k] = lax.ppermute(blocks[k], "chan", ahead(k))
            sent.append(lax.dynamic_index_in_dim(blocks[k], 1 - core, 0))
        early = lax.ppermute(jnp.concatenate(sent[:-1]), "chan", swap)
        last = lax.ppermute(sent[-1], "chan", swap)
        return call(
            functools.partial(unpack_kernel, arrival),
            jax.ShapeDtypeStruct(volume.shape, BF16),
            [early, last, *blocks],
            [pltpu.VMEM((chan, rows, width, lanes), BF16)],
            name="unpack_rows",
        )

    placed = (P("chan", "space", None, None), P(), P(), P(), P())
    return jax.shard_map(
        per_device,
        mesh=mesh,
        in_specs=placed,
        out_specs=P("chan", "space", None, None),
        check_vma=False,
    )
```

```python
import jax
import jax.numpy as jnp
from jax import lax
from jax.experimental import pallas as pl
from jax.experimental.pallas import tpu as pltpu
from jax.sharding import PartitionSpec as P

BF16 = jnp.bfloat16
F32 = jnp.float32
CORES = 2
RIM = 2
PARAMS = pltpu.CompilerParams(vmem_limit_bytes=24 * 1024 * 1024)
VMEM = pl.BlockSpec(memory_space=pltpu.VMEM)


def my_group():
    return lax.axis_index("chan") // CORES


def my_core():
    return lax.axis_index("chan") % CORES


def along_lanes(total, lanes):
    chans = total.shape[0] // 3
    lane = lax.broadcasted_iota(jnp.int32, (chans, lanes), 1)
    low = pltpu.roll(total[:chans], 1, 1)
    high = pltpu.roll(total[2 * chans :], lanes - 1, 1)
    return (
        total[chans : 2 * chans]
        + jnp.where(lane == 0, 0.0, low)
        + jnp.where(lane == lanes - 1, 0.0, high)
    )


def conv_rows(get, planes, weight, store, rows, lanes):
    for start in range(0, rows, 2):
        parts = []
        for a in range(planes):
            for e in range(3):
                pair = [get(a, start + e + n) for n in range(2)]
                parts.append(jnp.concatenate(pair, axis=1))
        stacked = jnp.concatenate(parts, axis=0)
        total = jnp.dot(weight, stacked, preferred_element_type=F32)
        for n in range(2):
            store(start + n, along_lanes(total[:, n * lanes : (n + 1) * lanes], lanes))


def pack_kernel(volume_ref, *refs):
    outs, rows_ref = refs[:-1], refs[-1]
    width, _, length, lanes = volume_ref.shape
    groups = len(outs)
    rows = length // groups
    edge = jnp.zeros((RIM, width, lanes), BF16)
    rows_ref[:RIM] = edge
    rows_ref[RIM + length :] = edge
    turned = jnp.swapaxes(volume_ref[:, 0].astype(F32), 0, 1)
    rows_ref[RIM : RIM + length] = turned.astype(BF16)
    for k in range(groups):
        target = lax.rem(my_group() + k, groups)
        outs[k][0] = rows_ref[pl.ds(target * rows, rows + 2 * RIM)]


def gather_rows(kept_ref, other_ref, joined_ref):
    core = my_core()
    groups, rows, width, lanes = other_ref.shape
    offset = core * (kept_ref.shape[1] - rows)
    for row in range(rows):
        parts = []
        for g in range(groups):
            kept = kept_ref[g, offset + row]
            other = other_ref[g, row]
            parts += [jnp.where(core == 0, kept, other), jnp.where(core == 0, other, kept)]
        joined_ref[row] = jnp.concatenate(parts, axis=0)


def rows_of(ref, masked):
    def get(_, row):
        value = ref[row]
        if masked:
            plane = lax.axis_index("space")
            edge = (plane == 0) | (plane == lax.axis_size("space") - 1)
            value = jnp.where(edge, jnp.zeros_like(value), value)
        return value

    return get


def own_kernel(plane_ref, weight_ref, out_ref):
    rows, _, lanes = out_ref.shape

    def store(row, value):
        out_ref[row] = value

    conv_rows(rows_of(plane_ref, False), 1, weight_ref[...], store, rows, lanes)


def near_kernel(plane_ref, weight_ref, before_ref, out_ref):
    rows, _, lanes = out_ref.shape

    def store(row, value):
        out_ref[row] = before_ref[row] + value

    weight = weight_ref[1 - lax.axis_index("space") % 2]
    conv_rows(rows_of(plane_ref, False), 1, weight, store, rows, lanes)


def first_own_kernel(kept_ref, other_ref, weight_ref, later_ref, bias_ref, out_ref, zero_ref, joined_ref):
    gather_rows(kept_ref, other_ref, joined_ref)
    own_kernel(joined_ref, weight_ref, out_ref)
    zero_ref[...] = jnp.zeros_like(zero_ref)


def first_near_kernel(kept_ref, other_ref, weight_ref, before_ref, out_ref, joined_ref):
    gather_rows(kept_ref, other_ref, joined_ref)
    near_kernel(joined_ref, weight_ref, before_ref, out_ref)


def first_far_kernel(kept_ref, other_ref, weight_ref, before_ref, bias_ref, out_ref, joined_ref):
    gather_rows(kept_ref, other_ref, joined_ref)
    rows, _, lanes = out_ref.shape
    block = lax.axis_index("chan")
    bias = bias_ref[...]

    def store(row, value):
        value = jnp.maximum(value + before_ref[row] + bias, 0.0)
        if row == 0:
            value = jnp.where(block == 0, 0.0, value)
        if row == rows - 1:
            value = jnp.where(block == lax.axis_size("chan") - 1, 0.0, value)
        out_ref[row] = value.astype(BF16)

    weight = weight_ref[lax.axis_index("space") % 2]
    conv_rows(rows_of(joined_ref, True), 1, weight, store, rows, lanes)


def far_kernel(plane_ref, weight_ref, before_ref, out_ref):
    rows, _, lanes = out_ref.shape

    def store(row, value):
        out_ref[row] = before_ref[row] + value

    weight = weight_ref[lax.axis_index("space") % 2]
    conv_rows(rows_of(plane_ref, True), 1, weight, store, rows, lanes)


def second_kernel(plane_ref, weight_ref, before_ref, bias_ref, *refs):
    outs, all_ref = refs[:-1], refs[-1]
    groups, cores, rows, width, lanes = all_ref.shape
    bias = bias_ref[...]

    def store(row, value):
        value = jnp.maximum(value + before_ref[row] + bias, 0.0).astype(BF16)
        for g in range(groups):
            for c in range(cores):
                at = (g * cores + c) * width
                all_ref[g, c, row] = value[at : at + width]

    weight = weight_ref[1 - lax.axis_index("space") % 2]
    conv_rows(rows_of(plane_ref, False), 1, weight, store, rows, lanes)
    for k in range(groups):
        outs[k][...] = all_ref[lax.rem(my_group() + k, groups)]


def unpack_kernel(swapped_ref, *refs):
    blocks, out_ref, rows_ref = refs[:-2], refs[-2], refs[-1]
    groups = len(blocks)
    _, rows, width, lanes = blocks[0].shape
    group, core = my_group(), my_core()
    for k in range(groups):
        source = lax.rem(group + groups - k, groups) * CORES
        rows_ref[source + core] = blocks[k][core]
        rows_ref[source + 1 - core] = swapped_ref[k]
    length = groups * CORES * rows
    turned = rows_ref[...].reshape(length, width, lanes).astype(F32)
    out_ref[:, 0] = jnp.swapaxes(turned, 0, 1).astype(BF16)


def arranged(weight):
    _, inner, outer = weight.shape
    taps = weight.reshape(3, 3, 3, inner, outer)
    own = taps[1].transpose(1, 3, 0, 2).reshape(3 * outer, 3 * inner)
    beside = taps[::2].transpose(0, 2, 4, 1, 3).reshape(2, 3 * outer, 3 * inner)
    return own, beside


def cost(rows, planes, full, lanes):
    flops = 2 * rows * lanes * full * full * 9 * planes
    return pl.CostEstimate(flops=flops, bytes_accessed=4_000_000, transcendentals=0)


def solution(mesh):
    space = mesh.shape["space"]
    chan = mesh.shape["chan"]
    groups = chan // CORES
    swap = [(i, i ^ 1) for i in range(chan)]

    near = [(i, i ^ 1) for i in range(space)]

    def far_partner(i, j):
        if i in (0, space - 1):
            return i * chan + (j ^ 1)
        return (((i - 1) ^ 1) + 1) * chan + j

    far = [(i * chan + j, far_partner(i, j)) for i in range(space) for j in range(chan)]

    order = sorted(range(1, groups), key=lambda k: abs(k - groups // 2))

    def ahead(k):
        return [(i, (i + CORES * k) % chan) for i in range(chan)]

    def call(kernel, shapes, inputs, scratch=(), **kwargs):
        single = not isinstance(shapes, list)
        return pl.pallas_call(
            kernel,
            out_shape=shapes,
            in_specs=[VMEM] * len(inputs),
            out_specs=VMEM if single else [VMEM] * len(shapes),
            scratch_shapes=scratch,
            compiler_params=PARAMS,
            **kwargs,
        )(*inputs)

    def per_device(volume, weight_one, bias_one, weight_two, bias_two):
        width, _, length, lanes = volume.shape
        full = width * chan
        rows = length // chan
        index = lax.axis_index("chan")
        group, core = index // CORES, index % CORES

        own_one, beside_one = arranged(weight_one)
        own_two, beside_two = arranged(weight_two)

        tall = CORES * rows + 2 * RIM
        pieces = call(
            pack_kernel,
            [jax.ShapeDtypeStruct((1, tall, width, lanes), BF16)] * groups,
            [volume],
            [pltpu.VMEM((length + 2 * RIM, width, lanes), BF16)],
            name="pack_rows",
        )
        kept = jnp.zeros((groups, tall, width, lanes), BF16)
        kept = lax.dynamic_update_slice_in_dim(kept, pieces[0], group, 0)
        for k in order:
            got = lax.ppermute(pieces[k], "chan", ahead(k))
            kept = lax.dynamic_update_slice_in_dim(kept, got, (group + groups - k) % groups, 0)

        def from_other_core(array, core):
            sent = lax.dynamic_slice_in_dim(array, (1 - core) * rows, rows + 2 * RIM, 1)
            return lax.ppermute(sent, "chan", swap)

        def halo(array):
            return lax.ppermute(array, ("space", "chan"), far), lax.ppermute(array, "space", near)

        partial = jax.ShapeDtypeStruct((rows + RIM, full, lanes), F32)
        joined = [pltpu.VMEM((rows + 2 * RIM, full, lanes), BF16)]
        work = cost(rows + RIM, 1, full, lanes)
        far_plane, near_plane = halo(kept)
        total, zero = call(
            first_own_kernel,
            [partial, jax.ShapeDtypeStruct((8, 128), jnp.int32)],
            [kept, from_other_core(kept, core), own_one, beside_one, bias_one[:, None]],
            joined,
            cost_estimate=work,
            name="first_own",
        )
        later_core = core + zero[0, 0]
        total = call(
            first_near_kernel,
            partial,
            [near_plane, from_other_core(near_plane, later_core), beside_one, total],
            joined,
            cost_estimate=work,
            name="first_near",
        )
        hidden = call(
            first_far_kernel,
            jax.ShapeDtypeStruct((rows + RIM, full, lanes), BF16),
            [far_plane, from_other_core(far_plane, later_core), beside_one, total, bias_one[:, None]],
            joined,
            cost_estimate=work,
            name="first_far",
        )

        partial = jax.ShapeDtypeStruct((rows, full, lanes), F32)
        work = cost(rows, 1, full, lanes)
        far_plane, near_plane = halo(hidden)
        total = call(own_kernel, partial, [hidden, own_two], cost_estimate=work, name="second_own")
        total = call(far_kernel, partial, [far_plane, beside_two, total], cost_estimate=work, name="second_far")
        blocks = call(
            second_kernel,
            [jax.ShapeDtypeStruct((CORES, rows, width, lanes), BF16)] * groups,
            [near_plane, beside_two, total, bias_two[:, None]],
            [pltpu.VMEM((groups, CORES, rows, width, lanes), BF16)],
            cost_estimate=work,
            name="second_near",
        )

        blocks = list(blocks)
        theirs = jnp.zeros((groups, rows, width, lanes), BF16)
        for k in [0, *order]:
            if k:
                blocks[k] = lax.ppermute(blocks[k], "chan", ahead(k))
            sent = lax.dynamic_index_in_dim(blocks[k], 1 - core, 0)
            theirs = lax.dynamic_update_slice_in_dim(theirs, sent, k, 0)
        swapped = lax.ppermute(theirs, "chan", swap)
        return call(
            unpack_kernel,
            jax.ShapeDtypeStruct(volume.shape, BF16),
            [swapped, *blocks],
            [pltpu.VMEM((chan, rows, width, lanes), BF16)],
            name="unpack_rows",
        )

    placed = (P("chan", "space", None, None), P(), P(), P(), P())
    return jax.shard_map(
        per_device,
        mesh=mesh,
        in_specs=placed,
        out_specs=P("chan", "space", None, None),
        check_vma=False,
    )
```
